256 devices in a mesh: sec: 4 (over y_lo, core), tile: 64 (over z, y_hi, x).
Axes of the slice: x: 4, y: 4 (y_hi: 2, y_lo: 2; y = y_hi * 2 + y_lo), z: 8, core: 2. Of those that a mesh axis runs over, the one named last changes fastest.
Arguments:
- surface: float32 [4, 4096, 2560], P('sec', 'tile'), may hold values from -6 to 6
- remap_weights: float32 [4096, 8, 4096], P('tile'), may hold values from -0.25 to 0.25
- src_tiles: int32 [4096, 8], P('tile'), may hold values from 0 to 12287, as said below
- block_count: int32 [4096], P('tile'), may hold values from 1 to 8, as said below
- land_sea: int32 [4096, 64], P('tile'), may hold values from 0 to 1
- exchange_coef: float32 [40], replicated, may hold values from 0.2 to 2
Outputs:
- section_flux: float32 [4, 4096, 2560], P('sec', 'tile')
The draws below stay inside these ranges and needn't reach their ends.
Inputs may be any that keep to these rules, and one draw needn't show every extreme that they name: `src_tiles`: every id names an atmosphere tile whose band (id mod 4096) // 64 lies within one band, cyclically, of the ocean tile's band t // 64; ids at k >= block_count[t] are ignored. `block_count`: some tile has 8 blocks.
All inputs are finite; a program needn't handle non-finite values.
Results may differ from the reference program's by a relative error of at most 0.0001.
Values sent between devices are 32-bit elements; how exact they have to be, the bound alone decides.
A program may use at most 128 MiB of HBM per device.

```python
import math
import jax
import jax.numpy as jnp
from jax import lax

FIELDS = 40
CELLS = 64
BLOCKS = 8
TILE_DEV = 64
SEC_TILES = 4096
ATM_SECS = 3
N_SEC = 4


def draw_src_tiles(key, part):
    key = jax.random.fold_in(key, 11)
    key_sec, key_move, key_row = jax.random.split(key, 3)
    bands = SEC_TILES // TILE_DEV
    band = (jnp.arange(SEC_TILES) // TILE_DEV)[:, None]
    section = jax.random.randint(key_sec, (SEC_TILES, BLOCKS), 0, ATM_SECS)
    moved = jax.random.randint(key_move, (SEC_TILES, BLOCKS), -1, 2)
    row_in = jax.random.randint(key_row, (SEC_TILES, BLOCKS), 0, TILE_DEV)
    near = (band + moved + bands) % bands
    return (section * SEC_TILES + near * TILE_DEV + row_in).astype(jnp.int32)


def draw_block_count(key, part):
    key = jax.random.fold_in(key, 12)
    key_top, key_full, key_cnt, key_pos = jax.random.split(key, 4)
    bands = SEC_TILES // TILE_DEV
    top = jax.random.randint(key_top, (bands,), 2, BLOCKS + 1)
    full_band = jax.random.randint(key_full, (), 0, bands)
    top = jnp.where(jnp.arange(bands) == full_band, BLOCKS, top)
    counts = jax.random.randint(key_cnt, (bands, TILE_DEV), 1, top[:, None] + 1)
    place = jax.random.randint(key_pos, (bands,), 0, TILE_DEV)
    counts = jnp.where(jnp.arange(TILE_DEV)[None, :] == place[:, None], top[:, None], counts)
    return counts.reshape(SEC_TILES).astype(jnp.int32)


def draw_land_sea(key, part):
    key = jax.random.fold_in(key, 13)
    key_share, key_cell = jax.random.split(key, 2)
    bands = SEC_TILES // TILE_DEV
    share = jax.random.randint(key_share, (bands,), 100, 1001)
    cell = jax.random.randint(key_cell, (bands, TILE_DEV, CELLS), 0, 1000)
    wet = jnp.where(cell < share[:, None, None], 1, 0)
    return wet.reshape(SEC_TILES, CELLS).astype(jnp.int32)


def level_of(key, shape, cuts, low, high):
    factor_of = 1.0
    for dim, parts in cuts:
        heights = jax.random.uniform(jax.random.fold_in(jax.random.fold_in(key, 6), dim), (parts,), jnp.float32, low / len(cuts), high / len(cuts))
        factor_of = factor_of * jnp.repeat(jnp.exp(heights), shape[dim] // parts).reshape((-1,) + (1,) * (len(shape) - 1 - dim))
    return factor_of


def centred(stream_key, dims, width, most, shards=(), kind=jnp.bfloat16):
    result = width * jax.random.normal(stream_key, dims, jnp.float32)
    if shards:
        result = result * level_of(stream_key, dims, shards, -0.22, 0.18)
    return jnp.clip(result, -most, most).astype(kind)


def setup_inputs(seed: int = 0) -> dict:
    seeds = jax.random.split(jax.random.key(seed), 7)
    return {
        "surface": centred(seeds[0], (N_SEC, SEC_TILES, FIELDS * CELLS), 1.0, 6.0, ((0, 4), (1, 64)), jnp.float32),
        "remap_weights": centred(seeds[1], (SEC_TILES, BLOCKS, CELLS * CELLS), (BLOCKS * CELLS) ** -0.5, 0.25, ((0, 64),), jnp.float32),
        "src_tiles": draw_src_tiles(jax.random.fold_in(seeds[6], 71), 0),
        "block_count": draw_block_count(jax.random.fold_in(seeds[6], 71), 0),
        "land_sea": draw_land_sea(jax.random.fold_in(seeds[6], 71), 0),
        "exchange_coef": jnp.clip(jnp.exp(jax.random.uniform(seeds[5], (FIELDS,), jnp.float32, math.log(0.2), math.log(2.0))), 0.2, 2.0),
    }


def reference(surface, remap_weights, src_tiles, block_count, land_sea, exchange_coef):
    wide = FIELDS * CELLS
    bands = SEC_TILES // TILE_DEV
    atm = surface[:ATM_SECS].reshape(ATM_SECS * SEC_TILES, wide)
    ocean = surface[ATM_SECS].reshape(SEC_TILES, FIELDS, CELLS)
    valid = jnp.arange(BLOCKS)[None, :] < block_count[:, None]
    weights = remap_weights.reshape(bands, TILE_DEV, BLOCKS, CELLS, CELLS)
    ids = src_tiles.reshape(bands, TILE_DEV, BLOCKS).astype(jnp.int32)
    valid_b = valid.reshape(bands, TILE_DEV, BLOCKS)

    def forward(args):
        band_ids, band_w, band_valid = args
        picked = atm[band_ids].reshape(TILE_DEV, BLOCKS, FIELDS, CELLS)
        picked = jnp.where(band_valid[:, :, None, None], picked, 0.0)
        return jnp.einsum('tkfc,tkcd->tfd', picked, band_w, precision=lax.Precision.HIGHEST)
    remapped = lax.map(forward, (ids, weights, valid_b)).reshape(SEC_TILES, FIELDS, CELLS)
    rel = remapped - ocean
    speed = jnp.sqrt(rel[:, 0] * rel[:, 0] + rel[:, 1] * rel[:, 1] + 0.25)
    stab = 1.0 + 0.5 * jnp.tanh(-rel[:, 2])
    land = land_sea.astype(jnp.float32)
    flux = exchange_coef[None, :, None] * (speed * stab * land)[:, None, :] * rel
    flux_b = flux.reshape(bands, TILE_DEV, FIELDS, CELLS)

    def backward(total, args):
        band_ids, band_w, band_valid, band_flux = args
        contrib = jnp.einsum('tfd,tkcd->tkfc', band_flux, band_w, precision=lax.Precision.HIGHEST)
        contrib = jnp.where(band_valid[:, :, None, None], contrib, 0.0)
        total = total.at[band_ids.reshape(-1)].add(contrib.reshape(TILE_DEV * BLOCKS, wide))
        return (total, None)
    start = jnp.zeros((ATM_SECS * SEC_TILES, wide), jnp.float32)
    back, unused = lax.scan(backward, start, (ids, weights, valid_b, flux_b))
    return jnp.concatenate([back.reshape(ATM_SECS, SEC_TILES, wide), flux.reshape(1, SEC_TILES, wide)], axis=0)
```

```python
import functools
import jax
import jax.numpy as jnp
from jax import lax
from jax.experimental import pallas as pl
from jax.experimental.pallas import tpu as pltpu
from jax.sharding import PartitionSpec as P

MESH = pl.DeviceIdType.MESH
FIELDS, CELLS, BLOCKS, TILES = 40, 64, 8, 64
WIDE = FIELDS * CELLS
BANDS, SECS = 64, 4
KEEP = 48
GIVE = TILES - KEEP
SLOTS = 3 * KEEP
PAIRS = TILES // 2
HALF = PAIRS // 2
CHUNKS = (16, 24)
W_PARTS = 8
f32, bf16 = jnp.float32, jnp.bfloat16


def split(x):
    hi = x.astype(bf16).astype(f32)
    return hi, x - hi


def kernel(x_ref, w_ref, idx_ref, col_ref, wet_ref, coef_ref, out_ref, *scratch):
    n = len(CHUNKS)
    (wraw, wp, mix, hot, cb, fac, rel, fin) = scratch[:8]
    per = scratch[8 : 8 + 11 * n]
    (w_sem, own_sem, xs, xr, hs, hr, oss, orr, osl, s1s, s1r, ys, yr, s2s, s2r, bs, br, gs, gr) = (
        scratch[8 + 11 * n :]
    )
    band_in, part, sib, ysum, yrec, flux, oc, ocd, tot, rec, src = [
        [per[11 * i + j] for i in range(n)] for j in range(11)
    ]
    s, b = lax.axis_index("sec"), lax.axis_index("tile")
    core = lax.rem(s, 2)
    mate = s + 1 - 2 * core
    opp = lax.rem(s + 2, SECS)
    east, west = lax.rem(b + 1, BANDS), lax.rem(b + BANDS - 1, BANDS)
    taker = s == SECS - 1
    lane = lax.broadcasted_iota(jnp.int32, (1, 128), 1)
    low = lane < CELLS
    starts = [sum(CHUNKS[:i]) for i in range(n)]

    def remote(a, z, ss, rs, to):
        return pltpu.make_async_remote_copy(
            src_ref=a, dst_ref=z, send_sem=ss, recv_sem=rs, device_id=to, device_id_type=MESH
        )

    def lanes(i):
        return pl.ds(starts[i] * CELLS, CHUNKS[i] * CELLS)

    per_w = TILES // W_PARTS
    w_copy = [
        pltpu.make_async_copy(
            w_ref.at[pl.ds(i * per_w, per_w)], wraw.at[pl.ds(i * per_w, per_w)], w_sem.at[i]
        )
        for i in range(W_PARTS)
    ]
    keep_rows, give_rows = pl.ds(0, KEEP), pl.ds(KEEP, GIVE)
    own_copy = [
        pltpu.make_async_copy(x_ref.at[0, keep_rows, lanes(i)], band_in[i].at[1], own_sem.at[i])
        for i in range(n)
    ]

    def to_neighbours(i, block):
        return (
            remote(block, band_in[i].at[0], xs.at[i, 0], xr.at[i, 0], (s, east)),
            remote(block, band_in[i].at[2], xs.at[i, 1], xr.at[i, 1], (s, west)),
        )

    def hand_over(i, who):
        return remote(
            x_ref.at[0, give_rows, lanes(i)],
            band_in[i].at[1, pl.ds(pl.multiple_of(who * GIVE, GIVE), GIVE)],
            hs.at[i],
            hr.at[i, who],
            (SECS - 1, b),
        )

    def ocean_to(i, who):
        return remote(
            x_ref.at[0, pl.ds((who % 2) * 2 * HALF, 2 * HALF), lanes(i)],
            oc[i],
            oss.at[i, who],
            orr.at[i],
            (who, b),
        )

    def ocean_own(i):
        return pltpu.make_async_copy(
            x_ref.at[0, pl.ds(2 * HALF, 2 * HALF), lanes(i)], oc[i], osl.at[i]
        )

    for c in w_copy:
        c.start()

    @pl.when(jnp.logical_not(taker))
    def _():
        for i in range(n):
            own_copy[i].start()

    @pl.when(taker)
    def _():
        for i in range(n):
            ocean_own(i).start()

    barrier = pltpu.get_barrier_semaphore()
    for q in (1, 2, 3):
        pl.semaphore_signal(
            barrier, inc=1, device_id=(lax.rem(s + q, SECS), b), device_id_type=MESH
        )
    for z in (east, west):
        pl.semaphore_signal(barrier, inc=1, device_id=(s, z), device_id_type=MESH)
    pl.semaphore_wait(barrier, 5)

    @pl.when(jnp.logical_not(taker))
    def _():
        for i in range(n):
            hand_over(i, s).start()
            for c in to_neighbours(i, x_ref.at[0, keep_rows, lanes(i)]):
                c.start()

    def take_over(i):
        @pl.when(taker)
        def _():
            for who in range(SECS - 1):
                hand_over(i, who).wait_recv()
            for c in to_neighbours(i, band_in[i].at[1]):
                c.start()

    def prepare(t, _):
        for k in range(BLOCKS):
            hi, lo = split(wraw[t, pl.ds(k, CELLS // 2, stride=BLOCKS), :])
            left = jnp.where(low, hi, pltpu.roll(lo, CELLS, 1))
            right = jnp.where(low, pltpu.roll(hi, CELLS, 1), lo)
            mix[k, pl.ds(0, CELLS // 2, stride=2), :] = left
            mix[k, pl.ds(1, CELLS // 2, stride=2), :] = right
        for k in range(BLOCKS):
            wp[t, pl.ds(k * CELLS, CELLS), :] = mix[k].astype(bf16)
        return 0

    def prepare_part(i):
        w_copy[i].wait()
        lax.fori_loop(i * per_w, (i + 1) * per_w, prepare, 0)

    take_over(0)

    @pl.when(taker)
    def _():
        for i in range(n):
            for who in range(SECS - 1):
                ocean_to(i, who).start()

    for i in range(W_PARTS):
        prepare_part(i)
        if i + 1 < n:
            take_over(i + 1)

    rows = lax.broadcasted_iota(jnp.int32, (SLOTS, TILES * BLOCKS), 0)
    hot[...] = jnp.where(rows == col_ref[...], 1.0, 0.0).astype(bf16)

    def spread(view, count, F, dst, base):
        for g in range(count // 8):
            for j in range(F // 2):
                v = view[pl.ds(8 * g, 8), pl.ds(128 * j, 128)]
                r = pltpu.roll(v, CELLS, 1)
                at = (base + 8 * g) * F + 2 * j
                dst[pl.ds(at, 8, stride=F), :] = jnp.where(low, v, r)
                dst[pl.ds(at + 1, 8, stride=F), :] = jnp.where(low, r, v)

    def forward(i):
        F = CHUNKS[i]

        @pl.when(jnp.logical_not(taker))
        def _():
            own_copy[i].wait()

        src[i][SLOTS] = jnp.zeros((F, 128), f32)
        flat = src[i].reshape((SLOTS + 1) * F, 128)
        spread(band_in[i].at[1], KEEP, F, flat, KEEP)
        arrivals = to_neighbours(i, band_in[i].at[1])
        arrivals[0].wait_recv()
        spread(band_in[i].at[0], KEEP, F, flat, 0)
        arrivals[1].wait_recv()
        spread(band_in[i].at[2], KEEP, F, flat, 2 * KEEP)

        def pair(p, _):
            q = []
            for tp in range(2):
                t = 2 * p + tp
                cols = []
                for kp in range(BLOCKS // 2):
                    g0 = idx_ref[t * BLOCKS + 2 * kp]
                    g1 = idx_ref[t * BLOCKS + 2 * kp + 1]
                    cols.append(
                        jnp.where(
                            low,
                            src[i][g0],
                            src[i][g1],
                        )
                    )
                hi, lo = split(jnp.concatenate(cols, axis=1))
                lhs = jnp.concatenate([hi, lo], axis=0).astype(bf16)
                o = jnp.dot(lhs, wp[t], preferred_element_type=f32)
                q.append(o[:F] + pltpu.roll(o[:F], CELLS, 1) + o[F:])
            part[i][pl.ds(pl.multiple_of(p * F, 8), F), :] = jnp.where(
                low, q[0], pltpu.roll(q[1], CELLS, 1)
            )
            return 0

        first = (1 - core) * HALF
        lax.fori_loop(0, HALF, lambda u, c: pair(first + u, c), 0)
        sib_copy(i).start()
        lax.fori_loop(0, HALF, lambda u, c: pair(core * HALF + u, c), 0)

    def half_rows(i, which):
        size = HALF * CHUNKS[i]
        return pl.ds(pl.multiple_of(which * size, 8), size)

    def sib_copy(i):
        return remote(
            part[i].at[half_rows(i, 1 - core)], sib[i], s1s.at[i], s1r.at[i], (mate, b)
        )

    def y_copy(i):
        return remote(ysum[i], yrec[i], ys.at[i], yr.at[i], (opp, b))

    def flux_copy(i, which):
        at = flux[i].at[half_rows(i, which)]
        return remote(at, at, s2s.at[i], s2r.at[i], (mate, b))

    def reduce_chip(i):
        sib_copy(i).wait_recv()
        ysum[i][...] = part[i][half_rows(i, core), :] + sib[i][...]
        y_copy(i).start()

    def prepare_ocean(i):
        @pl.when(taker)
        def _():
            ocean_own(i).wait()

        @pl.when(jnp.logical_not(taker))
        def _():
            ocean_to(i, 0).wait_recv()

        spread(oc[i], 2 * HALF, CHUNKS[i], ocd[i], 0)

    def fluxes(i):
        F = CHUNKS[i]
        y_copy(i).wait_recv()

        def relative(u, _):
            at = pl.ds(pl.multiple_of(u * F, 8), F)
            a = ocd[i][pl.ds(pl.multiple_of(2 * u * F, 8), F), :]
            z = ocd[i][pl.ds(pl.multiple_of((2 * u + 1) * F, 8), F), :]
            rel[at, :] = ysum[i][at, :] + yrec[i][at, :] - jnp.where(low, a, z)
            return 0

        lax.fori_loop(0, HALF, relative, 0)
        if i == 0:
            r0, r1, r2 = [rel[pl.ds(f, HALF, stride=F), :] for f in range(3)]
            speed = jnp.sqrt(r0 * r0 + r1 * r1 + 0.25)
            stab = 1.0 + 0.5 * jnp.tanh(-r2)
            wet = wet_ref[pl.ds(pl.multiple_of(core * HALF, 8), HALF), :]
            fac[...] = speed * stab * wet
        coef = jnp.broadcast_to(coef_ref[pl.ds(starts[i], F), :], (F, 128))

        def scale(u, _):
            at = pl.ds(pl.multiple_of(u * F, 8), F)
            to = pl.ds(pl.multiple_of((core * HALF + u) * F, 8), F)
            flux[i][to, :] = coef * fac[pl.ds(u, 1), :] * rel[at, :]
            return 0

        lax.fori_loop(0, HALF, scale, 0)
        flux_copy(i, core).start()

    def back_copies(i):
        return (
            remote(tot[i].at[0], rec[i].at[1], bs.at[i, 0], br.at[i, 1], (s, west)),
            remote(tot[i].at[2], rec[i].at[0], bs.at[i, 1], br.at[i, 0], (s, east)),
        )

    def backward(i):
        F = CHUNKS[i]
        flux_copy(i, 1 - core).wait_recv()

        def pair(p, _):
            v = flux[i][pl.ds(pl.multiple_of(p * F, 8), F), :]
            r = pltpu.roll(v, CELLS, 1)
            for tp in range(2):
                t = 2 * p + tp
                hi, lo = split(jnp.where(low, v, r) if tp == 0 else jnp.where(low, r, v))
                lhs = jnp.concatenate([hi, lo], axis=0).astype(bf16)
                o = lax.dot_general(
                    lhs, wp[t], (((1,), (1,)), ((), ())), preferred_element_type=f32
                )
                o = o[:F] + o[F:]
                for kp in range(BLOCKS // 2):
                    at = pl.multiple_of((t * (BLOCKS // 2) + kp) * F, 8)
                    cb[pl.ds(at, F), :] = o[:, 128 * kp : 128 * kp + 128]
            return 0

        lax.fori_loop(0, PAIRS, pair, 0)

        def gather(j, _):
            count = TILES * BLOCKS // 2
            x0 = cb[pl.ds(2 * j, count, stride=F), :]
            x1 = cb[pl.ds(2 * j + 1, count, stride=F), :]
            top = jnp.where(low, x0, pltpu.roll(x1, CELLS, 1))
            bottom = jnp.where(low, pltpu.roll(x0, CELLS, 1), x1)
            hi, lo = split(jnp.concatenate([top, bottom], axis=0))
            rhs = jnp.concatenate([hi, lo], axis=1).astype(bf16)
            o = jnp.dot(hot[...], rhs, preferred_element_type=f32)
            o = o[:, :128] + o[:, 128:]
            at = pl.ds(pl.multiple_of(128 * j, 128), 128)
            for z in range(3):
                tot[i][z, :, at] = o[z * KEEP : (z + 1) * KEEP]
            return 0

        lax.fori_loop(0, F // 2, gather, 0)
        for c in back_copies(i):
            c.start()

    def give_back(i, who):
        return remote(
            fin.at[pl.ds(GIVE * who, GIVE), lanes(i)],
            out_ref.at[0, pl.ds(KEEP, GIVE), lanes(i)],
            gs.at[i, who],
            gr.at[i],
            (who, b),
        )

    def ocean_out(i):
        F = CHUNKS[i]
        for g in range(PAIRS // 8):
            for j in range(F // 2):
                x0 = flux[i][pl.ds(8 * g * F + 2 * j, 8, stride=F), :]
                x1 = flux[i][pl.ds(8 * g * F + 2 * j + 1, 8, stride=F), :]
                at = g * (FIELDS // 2) + starts[i] // 2 + j
                buf = mix.at[at % 8]
                buf[pl.ds(0, 8, stride=2), :] = jnp.where(low, x0, pltpu.roll(x1, CELLS, 1))
                buf[pl.ds(1, 8, stride=2), :] = jnp.where(low, pltpu.roll(x0, CELLS, 1), x1)
                out_ref[0, pl.ds(16 * g, 16), pl.ds(starts[i] * CELLS + 128 * j, 128)] = buf[
                    pl.ds(0, 16), :
                ]

    def finish(i):
        for c in back_copies(i):
            c.wait_recv()

        @pl.when(jnp.logical_not(taker))
        def _():
            out_ref[0, keep_rows, lanes(i)] = tot[i][1] + rec[i][0] + rec[i][1]

        @pl.when(taker)
        def _():
            fin[:, lanes(i)] = tot[i][1] + rec[i][0] + rec[i][1]
            for who in range(SECS - 1):
                give_back(i, who).start()

    for i in range(n):
        forward(i)
        prepare_ocean(i)
        reduce_chip(i)
    for i in range(n):
        fluxes(i)
        backward(i)

    @pl.when(taker)
    def _():
        for i in range(n):
            ocean_out(i)

    for i in range(n):
        finish(i)

    for i in range(n):
        for c in to_neighbours(i, band_in[i].at[1]):
            c.wait_send()
        sib_copy(i).wait_send()
        y_copy(i).wait_send()
        flux_copy(i, core).wait_send()
        for c in back_copies(i):
            c.wait_send()

    @pl.when(taker)
    def _():
        for i in range(n):
            for who in range(SECS - 1):
                ocean_to(i, who).wait_send()
                give_back(i, who).wait_send()

    @pl.when(jnp.logical_not(taker))
    def _():
        for i in range(n):
            hand_over(i, s).wait_send()
            give_back(i, 0).wait_recv()


def on_device(surface, remap_weights, src_tiles, block_count, land_sea, exchange_coef):
    n = len(CHUNKS)
    band, section = lax.axis_index("tile"), lax.axis_index("sec")
    valid = jnp.arange(BLOCKS)[None, :] < block_count[:, None]
    source_sec = src_tiles // (BANDS * TILES)
    within = src_tiles % (BANDS * TILES)
    slot = (within // TILES - band + 1 + BANDS) % BANDS
    row = within % TILES
    kept = row < KEEP
    owner = jnp.where(kept, source_sec, SECS - 1)
    local = jnp.where(kept, row, source_sec * GIVE + row - KEEP)
    index = jnp.where(valid & (owner == section), slot * KEEP + local, SLOTS)
    columns = index.reshape(TILES, BLOCKS // 2, 2).transpose(2, 0, 1).reshape(1, TILES * BLOCKS)
    wet = land_sea.astype(f32).reshape(PAIRS, 2 * CELLS)
    weights = (
        remap_weights.reshape(TILES, BLOCKS, CELLS // 2, 128)
        .transpose(0, 2, 1, 3)
        .reshape(TILES, BLOCKS * CELLS // 2, 128)
    )
    top = max(CHUNKS)
    scratch = [
        pltpu.VMEM((TILES, BLOCKS * CELLS // 2, 128), f32),
        pltpu.VMEM((TILES, BLOCKS * CELLS, 128), bf16),
        pltpu.VMEM((BLOCKS, CELLS, 128), f32),
        pltpu.VMEM((SLOTS, TILES * BLOCKS), bf16),
        pltpu.VMEM((TILES * BLOCKS // 2 * top, 128), f32),
        pltpu.VMEM((HALF, 128), f32),
        pltpu.VMEM((HALF * top, 128), f32),
        pltpu.VMEM((KEEP, WIDE), f32),
    ]
    for F in CHUNKS:
        scratch += [
            pltpu.VMEM((3, KEEP, F * CELLS), f32),
            pltpu.VMEM((PAIRS * F, 128), f32),
            pltpu.VMEM((HALF * F, 128), f32),
            pltpu.VMEM((HALF * F, 128), f32),
            pltpu.VMEM((HALF * F, 128), f32),
            pltpu.VMEM((PAIRS * F, 128), f32),
            pltpu.VMEM((2 * HALF, F * CELLS), f32),
            pltpu.VMEM((2 * HALF * F, 128), f32),
            pltpu.VMEM((3, KEEP, F * CELLS), f32),
            pltpu.VMEM((2, KEEP, F * CELLS), f32),
            pltpu.VMEM((SLOTS + 1, F, 128), f32),
        ]
    sem = pltpu.SemaphoreType.DMA
    scratch += [
        sem((W_PARTS,)),
        sem((n,)),
        sem((n, 2)),
        sem((n, 2)),
        sem((n,)),
        sem((n, SECS - 1)),
        sem((n, SECS - 1)),
        sem((n,)),
        sem((n,)),
        sem((n,)),
        sem((n,)),
        sem((n,)),
        sem((n,)),
        sem((n,)),
        sem((n,)),
        sem((n, 2)),
        sem((n, 2)),
        sem((n, SECS - 1)),
        sem((n,)),
    ]
    vmem = pl.BlockSpec(memory_space=pltpu.VMEM)
    anywhere = pl.BlockSpec(memory_space=pl.ANY)
    smem = pl.BlockSpec(memory_space=pltpu.SMEM)
    return pl.pallas_call(
        kernel,
        out_shape=jax.ShapeDtypeStruct((1, TILES, WIDE), f32),
        in_specs=[anywhere, anywhere, smem, vmem, vmem, vmem],
        out_specs=vmem,
        scratch_shapes=scratch,
        compiler_params=pltpu.CompilerParams(
            collective_id=0, has_side_effects=True, vmem_limit_bytes=56 * 2**20
        ),
    )(surface, weights, index.reshape(-1), columns, wet, exchange_coef[:, None])


def solution(mesh):
    placed = (
        P("sec", "tile", None),
        P("tile", None, None),
        P("tile", None),
        P("tile"),
        P("tile", None),
        P(),
    )
    return jax.shard_map(
        on_device, mesh=mesh, in_specs=placed, out_specs=P("sec", "tile", None), check_vma=False
    )
```

```python
import functools
import jax
import jax.numpy as jnp
from jax import lax
from jax.experimental import pallas as pl
from jax.experimental.pallas import tpu as pltpu
from jax.sharding import PartitionSpec as P

MESH = pl.DeviceIdType.MESH
FIELDS, CELLS, BLOCKS, TILES = 40, 64, 8, 64
WIDE = FIELDS * CELLS
BANDS, SECS = 64, 4
KEEP = 48
GIVE = TILES - KEEP
SLOTS = 3 * KEEP
PAIRS = TILES // 2
HALF = PAIRS // 2
CHUNKS = (16, 24)
W_PARTS = 8
RING = 4
f32, bf16 = jnp.float32, jnp.bfloat16


def split(x):
    hi = x.astype(bf16).astype(f32)
    return hi, x - hi


def kernel(x_ref, w_ref, ids_ref, used_ref, land_ref, coef_ref, out_ref, *scratch):
    n = len(CHUNKS)
    (wraw, wp, mix, hot, cb, fac, rel, fin) = scratch[:8]
    (ids, used, land, coef_in, index, idx, wet, coef) = scratch[8:16]
    per = scratch[16 : 16 + 11 * n]
    (small, w_sem, own_sem, xs, xr, hs, hr, oss, orr, osl, s1s, s1r, ys, yr, s2s, s2r, bs, br, gs, gr) = (
        scratch[16 + 11 * n :]
    )
    band_in, part, sib, ysum, yrec, flux, oc, ocd, tot, rec, src = [
        [per[11 * i + j] for i in range(n)] for j in range(11)
    ]
    s, b = lax.axis_index("sec"), lax.axis_index("tile")
    core = lax.rem(s, 2)
    mate = s + 1 - 2 * core
    opp = lax.rem(s + 2, SECS)
    east, west = lax.rem(b + 1, BANDS), lax.rem(b + BANDS - 1, BANDS)
    taker = s == SECS - 1
    x = lax.rem(b, RING)
    east_sec = jnp.where(x == RING - 1, opp, s)
    west_sec = jnp.where(x == 0, opp, s)
    lane = lax.broadcasted_iota(jnp.int32, (1, 128), 1)
    low = lane < CELLS
    starts = [sum(CHUNKS[:i]) for i in range(n)]

    def remote(a, z, ss, rs, to):
        return pltpu.make_async_remote_copy(
            src_ref=a, dst_ref=z, send_sem=ss, recv_sem=rs, device_id=to, device_id_type=MESH
        )

    def lanes(i):
        return pl.ds(starts[i] * CELLS, CHUNKS[i] * CELLS)

    per_w = TILES // W_PARTS
    w_copy = [
        pltpu.make_async_copy(
            w_ref.at[pl.ds(i * per_w, per_w)], wraw.at[pl.ds(i * per_w, per_w)], w_sem.at[i]
        )
        for i in range(W_PARTS)
    ]
    keep_rows, give_rows = pl.ds(0, KEEP), pl.ds(KEEP, GIVE)
    own_copy = [
        pltpu.make_async_copy(x_ref.at[0, keep_rows, lanes(i)], band_in[i].at[1], own_sem.at[i])
        for i in range(n)
    ]

    def to_neighbours(i, block):
        return (
            remote(block, band_in[i].at[0], xs.at[i, 0], xr.at[i, 0], (east_sec, east)),
            remote(block, band_in[i].at[2], xs.at[i, 1], xr.at[i, 1], (west_sec, west)),
        )

    def hand_over(i, who):
        return remote(
            x_ref.at[0, give_rows, lanes(i)],
            band_in[i].at[1, pl.ds(pl.multiple_of(who * GIVE, GIVE), GIVE)],
            hs.at[i],
            hr.at[i, who],
            (SECS - 1, b),
        )

    def ocean_to(i, who, z):
        return remote(
            x_ref.at[0, pl.ds((who % 2) * HALF + z * PAIRS, HALF), lanes(i)],
            oc[i].at[pl.ds(z * HALF, HALF)],
            oss.at[i, who, z],
            orr.at[i, z],
            (who, b),
        )

    def ocean_own(i, z):
        return pltpu.make_async_copy(
            x_ref.at[0, pl.ds(HALF + z * PAIRS, HALF), lanes(i)],
            oc[i].at[pl.ds(z * HALF, HALF)],
            osl.at[i, z],
        )

    tables = [
        pltpu.make_async_copy(a, z, small.at[j])
        for j, (a, z) in enumerate(
            ((ids_ref, ids), (used_ref, used), (land_ref, land), (coef_ref, coef_in))
        )
    ]

    for c in tables:
        c.start()
    for c in w_copy:
        c.start()

    @pl.when(jnp.logical_not(taker))
    def _():
        for i in range(n):
            own_copy[i].start()

    @pl.when(taker)
    def _():
        for i in range(n):
            for z in range(2):
                ocean_own(i, z).start()

    barrier = pltpu.get_barrier_semaphore()
    for q in (1, 2, 3):
        pl.semaphore_signal(
            barrier, inc=1, device_id=(lax.rem(s + q, SECS), b), device_id_type=MESH
        )
    for z in ((east_sec, east), (west_sec, west)):
        pl.semaphore_signal(barrier, inc=1, device_id=z, device_id_type=MESH)
    pl.semaphore_wait(barrier, 5)

    @pl.when(jnp.logical_not(taker))
    def _():
        for i in range(n):
            hand_over(i, s).start()
        for i in range(n):
            for c in to_neighbours(i, x_ref.at[0, keep_rows, lanes(i)]):
                c.start()

    def take_over(i):
        @pl.when(taker)
        def _():
            for who in range(SECS - 1):
                hand_over(i, who).wait_recv()
            for c in to_neighbours(i, band_in[i].at[1]):
                c.start()

    def prepare(t, _):
        for k in range(BLOCKS):
            hi, lo = split(wraw[t, pl.ds(k, CELLS // 2, stride=BLOCKS), :])
            left = jnp.where(low, hi, pltpu.roll(lo, CELLS, 1))
            right = jnp.where(low, pltpu.roll(hi, CELLS, 1), lo)
            mix[k, pl.ds(0, CELLS // 2, stride=2), :] = left
            mix[k, pl.ds(1, CELLS // 2, stride=2), :] = right
        for k in range(BLOCKS):
            wp[t, pl.ds(k * CELLS, CELLS), :] = mix[k].astype(bf16)
        return 0

    def prepare_part(i):
        w_copy[i].wait()
        lax.fori_loop(i * per_w, (i + 1) * per_w, prepare, 0, unroll=4)

    take_over(0)

    @pl.when(taker)
    def _():
        for i in range(n):
            for who in range(SECS - 1):
                for z in range(2):
                    ocean_to(i, who, z).start()

    for c in tables:
        c.wait()
    sec_tiles = BANDS * TILES
    source = ids[...] // sec_tiles
    within = ids[...] % sec_tiles
    slot = (within // TILES - b + 1 + BANDS) % BANDS
    row = within % TILES
    kept = row < KEEP
    owner = jnp.where(kept, source, SECS - 1)
    local = jnp.where(kept, row, source * GIVE + row - KEEP)
    holder = jnp.where(slot == 0, west_sec, jnp.where(slot == 2, east_sec, s))
    valid = lax.broadcasted_iota(jnp.int32, (BLOCKS, TILES), 0) < used[...]
    named = jnp.where(valid & (owner == holder), slot * KEEP + local, SLOTS)
    index[...] = jnp.concatenate([named, named], axis=1)
    to_smem = pltpu.make_async_copy(index, idx, small.at[len(tables)])
    to_smem.start()
    rows = lax.broadcasted_iota(jnp.int32, (SLOTS, 128), 0)
    for kpar in range(2):
        for h in range(2):
            k = 4 * h + kpar
            named = jnp.where(low, index[pl.ds(k, 1), :], index[pl.ds(k + 2, 1), :])
            at = pl.ds(128 * (2 * kpar + h), 128)
            hot[:, at] = jnp.where(rows == named, 1.0, 0.0).astype(bf16)
    dry = land[...].astype(f32)
    wet[...] = jnp.concatenate([dry[:PAIRS], dry[PAIRS:]], axis=1)
    square = [lax.broadcasted_iota(jnp.int32, (FIELDS, FIELDS), d) for d in range(2)]
    diagonal = jnp.where(square[0] == square[1], coef_in[...], 0.0)
    coef[...] = jnp.broadcast_to(jnp.sum(diagonal, axis=1, keepdims=True), (FIELDS, 128))

    for i in range(W_PARTS):
        prepare_part(i)
        if i + 1 < n:
            take_over(i + 1)
    to_smem.wait()

    def spread(view, count, F, dst, base):
        for g in range(count // 8):
            for j in range(F // 2):
                v = view[pl.ds(8 * g, 8), pl.ds(128 * j, 128)]
                r = pltpu.roll(v, CELLS, 1)
                at = (base + 8 * g) * F + 2 * j
                dst[pl.ds(at, 8, stride=F), :] = jnp.where(low, v, r)
                dst[pl.ds(at + 1, 8, stride=F), :] = jnp.where(low, r, v)

    def forward(i):
        F = CHUNKS[i]

        @pl.when(jnp.logical_not(taker))
        def _():
            own_copy[i].wait()

        src[i][SLOTS] = jnp.zeros((F, 128), f32)
        flat = src[i].reshape((SLOTS + 1) * F, 128)
        spread(band_in[i].at[1], KEEP, F, flat, KEEP)
        arrivals = to_neighbours(i, band_in[i].at[1])
        arrivals[0].wait_recv()
        spread(band_in[i].at[0], KEEP, F, flat, 0)
        arrivals[1].wait_recv()
        spread(band_in[i].at[2], KEEP, F, flat, 2 * KEEP)

        def pair(p, _):
            q = []
            for tp in range(2):
                t = p + PAIRS * tp
                cols = []
                for kp in range(BLOCKS // 2):
                    g0 = idx[2 * kp, t]
                    g1 = idx[2 * kp + 1, t]
                    cols.append(
                        jnp.where(
                            low,
                            src[i][g0],
                            src[i][g1],
                        )
                    )
                hi, lo = split(jnp.concatenate(cols, axis=1))
                lhs = jnp.concatenate([hi, lo], axis=0).astype(bf16)
                o = jnp.dot(lhs, wp[t], preferred_element_type=f32)
                q.append(o[:F] + pltpu.roll(o[:F], CELLS, 1) + o[F:])
            part[i][pl.ds(pl.multiple_of(p * F, 8), F), :] = jnp.where(
                low, q[0], pltpu.roll(q[1], CELLS, 1)
            )
            return 0

        first = (1 - core) * HALF
        lax.fori_loop(0, HALF, lambda u, c: pair(first + u, c), 0, unroll=8)
        sib_copy(i).start()
        lax.fori_loop(0, HALF, lambda u, c: pair(core * HALF + u, c), 0, unroll=8)

    def half_rows(i, which):
        size = HALF * CHUNKS[i]
        return pl.ds(pl.multiple_of(which * size, 8), size)

    def sib_copy(i):
        return remote(
            part[i].at[half_rows(i, 1 - core)], sib[i], s1s.at[i], s1r.at[i], (mate, b)
        )

    def y_copy(i):
        return remote(ysum[i], yrec[i], ys.at[i], yr.at[i], (opp, b))

    def flux_copy(i, which):
        at = flux[i].at[half_rows(i, which)]
        return remote(at, at, s2s.at[i], s2r.at[i], (mate, b))

    def reduce_chip(i):
        sib_copy(i).wait_recv()
        ysum[i][...] = part[i][half_rows(i, core), :] + sib[i][...]
        y_copy(i).start()

    def prepare_ocean(i):
        @pl.when(taker)
        def _():
            for z in range(2):
                ocean_own(i, z).wait()

        @pl.when(jnp.logical_not(taker))
        def _():
            for z in range(2):
                ocean_to(i, 0, z).wait_recv()

        spread(oc[i], 2 * HALF, CHUNKS[i], ocd[i], 0)

    def fluxes(i):
        F = CHUNKS[i]
        y_copy(i).wait_recv()

        def relative(u, _):
            at = pl.ds(pl.multiple_of(u * F, 8), F)
            a = ocd[i][pl.ds(pl.multiple_of(u * F, 8), F), :]
            z = ocd[i][pl.ds(pl.multiple_of((HALF + u) * F, 8), F), :]
            rel[at, :] = ysum[i][at, :] + yrec[i][at, :] - jnp.where(low, a, z)
            return 0

        lax.fori_loop(0, HALF, relative, 0)
        if i == 0:
            r0, r1, r2 = [rel[pl.ds(f, HALF, stride=F), :] for f in range(3)]
            speed = jnp.sqrt(r0 * r0 + r1 * r1 + 0.25)
            stab = 1.0 + 0.5 * jnp.tanh(-r2)
            fac[...] = speed * stab * wet[pl.ds(pl.multiple_of(core * HALF, 8), HALF), :]
        exchange = coef[pl.ds(starts[i], F), :]

        def scale(u, _):
            at = pl.ds(pl.multiple_of(u * F, 8), F)
            to = pl.ds(pl.multiple_of((core * HALF + u) * F, 8), F)
            flux[i][to, :] = exchange * fac[pl.ds(u, 1), :] * rel[at, :]
            return 0

        lax.fori_loop(0, HALF, scale, 0)
        flux_copy(i, core).start()

    def back_copies(i):
        return (
            remote(tot[i].at[0], rec[i].at[1], bs.at[i, 0], br.at[i, 1], (west_sec, west)),
            remote(tot[i].at[2], rec[i].at[0], bs.at[i, 1], br.at[i, 0], (east_sec, east)),
        )

    def backward(i):
        F = CHUNKS[i]
        flux_copy(i, 1 - core).wait_recv()

        def pair(p, _):
            v = flux[i][pl.ds(pl.multiple_of(p * F, 8), F), :]
            r = pltpu.roll(v, CELLS, 1)
            for tp in range(2):
                t = p + PAIRS * tp
                hi, lo = split(jnp.where(low, v, r) if tp == 0 else jnp.where(low, r, v))
                lhs = jnp.concatenate([hi, lo], axis=0).astype(bf16)
                o = lax.dot_general(
                    lhs, wp[t], (((1,), (1,)), ((), ())), preferred_element_type=f32
                )
                o = o[:F] + o[F:]
                for kp in range(BLOCKS // 2):
                    at = pl.multiple_of((kp * TILES + t) * F, 8)
                    cb[pl.ds(at, F), :] = o[:, 128 * kp : 128 * kp + 128]
            return 0

        lax.fori_loop(0, PAIRS, pair, 0, unroll=8)

        def gather(j, _):
            count = TILES * BLOCKS // 2
            x0 = cb[pl.ds(2 * j, count, stride=F), :]
            x1 = cb[pl.ds(2 * j + 1, count, stride=F), :]
            top = jnp.where(low, x0, pltpu.roll(x1, CELLS, 1))
            bottom = jnp.where(low, pltpu.roll(x0, CELLS, 1), x1)
            hi, lo = split(jnp.concatenate([top, bottom], axis=0))
            rhs = jnp.concatenate([hi, lo], axis=1).astype(bf16)
            o = jnp.dot(hot[...], rhs, preferred_element_type=f32)
            o = o[:, :128] + o[:, 128:]
            at = pl.ds(pl.multiple_of(128 * j, 128), 128)
            for z in range(3):
                tot[i][z, :, at] = o[z * KEEP : (z + 1) * KEEP]
            return 0

        lax.fori_loop(0, F // 2, gather, 0, unroll=4)
        for c in back_copies(i):
            c.start()

    def give_back(i, who):
        return remote(
            fin.at[pl.ds(GIVE * who, GIVE), lanes(i)],
            out_ref.at[0, pl.ds(KEEP, GIVE), lanes(i)],
            gs.at[i, who],
            gr.at[i],
            (who, b),
        )

    def ocean_out(i):
        F = CHUNKS[i]
        for g in range(PAIRS // 8):
            for j in range(F // 2):
                x0 = flux[i][pl.ds(8 * g * F + 2 * j, 8, stride=F), :]
                x1 = flux[i][pl.ds(8 * g * F + 2 * j + 1, 8, stride=F), :]
                at = pl.ds(starts[i] * CELLS + 128 * j, 128)
                out_ref[0, pl.ds(8 * g, 8), at] = jnp.where(low, x0, pltpu.roll(x1, CELLS, 1))
                out_ref[0, pl.ds(PAIRS + 8 * g, 8), at] = jnp.where(
                    low, pltpu.roll(x0, CELLS, 1), x1
                )

    def finish(i):
        for c in back_copies(i):
            c.wait_recv()

        @pl.when(jnp.logical_not(taker))
        def _():
            out_ref[0, keep_rows, lanes(i)] = tot[i][1] + rec[i][0] + rec[i][1]

        @pl.when(taker)
        def _():
            fin[:, lanes(i)] = tot[i][1] + rec[i][0] + rec[i][1]
            for who in range(SECS - 1):
                give_back(i, who).start()

    for i in range(n):
        forward(i)
        prepare_ocean(i)
        reduce_chip(i)
    for i in range(n):
        fluxes(i)
        backward(i)

    @pl.when(taker)
    def _():
        for i in range(n):
            ocean_out(i)

    for i in range(n):
        finish(i)

    for i in range(n):
        for c in to_neighbours(i, band_in[i].at[1]):
            c.wait_send()
        sib_copy(i).wait_send()
        y_copy(i).wait_send()
        flux_copy(i, core).wait_send()
        for c in back_copies(i):
            c.wait_send()

    @pl.when(taker)
    def _():
        for i in range(n):
            for who in range(SECS - 1):
                for z in range(2):
                    ocean_to(i, who, z).wait_send()
                give_back(i, who).wait_send()

    @pl.when(jnp.logical_not(taker))
    def _():
        for i in range(n):
            hand_over(i, s).wait_send()
            give_back(i, 0).wait_recv()


def on_device(surface, remap_weights, src_tiles, block_count, land_sea, exchange_coef):
    n = len(CHUNKS)
    weights = (
        remap_weights.reshape(TILES, BLOCKS, CELLS // 2, 128)
        .transpose(0, 2, 1, 3)
        .reshape(TILES, BLOCKS * CELLS // 2, 128)
    )
    top = max(CHUNKS)
    scratch = [
        pltpu.VMEM((TILES, BLOCKS * CELLS // 2, 128), f32),
        pltpu.VMEM((TILES, BLOCKS * CELLS, 128), bf16),
        pltpu.VMEM((BLOCKS, CELLS, 128), f32),
        pltpu.VMEM((SLOTS, TILES * BLOCKS), bf16),
        pltpu.VMEM((TILES * BLOCKS // 2 * top, 128), f32),
        pltpu.VMEM((HALF, 128), f32),
        pltpu.VMEM((HALF * top, 128), f32),
        pltpu.VMEM((KEEP, WIDE), f32),
        pltpu.VMEM((BLOCKS, TILES), jnp.int32),
        pltpu.VMEM((1, TILES), jnp.int32),
        pltpu.VMEM((TILES, CELLS), jnp.int32),
        pltpu.VMEM((1, FIELDS), f32),
        pltpu.VMEM((BLOCKS, 128), jnp.int32),
        pltpu.SMEM((BLOCKS, 128), jnp.int32),
        pltpu.VMEM((PAIRS, 128), f32),
        pltpu.VMEM((FIELDS, 128), f32),
    ]
    for F in CHUNKS:
        scratch += [
            pltpu.VMEM((3, KEEP, F * CELLS), f32),
            pltpu.VMEM((PAIRS * F, 128), f32),
            pltpu.VMEM((HALF * F, 128), f32),
            pltpu.VMEM((HALF * F, 128), f32),
            pltpu.VMEM((HALF * F, 128), f32),
            pltpu.VMEM((PAIRS * F, 128), f32),
            pltpu.VMEM((2 * HALF, F * CELLS), f32),
            pltpu.VMEM((2 * HALF * F, 128), f32),
            pltpu.VMEM((3, KEEP, F * CELLS), f32),
            pltpu.VMEM((2, KEEP, F * CELLS), f32),
            pltpu.VMEM((SLOTS + 1, F, 128), f32),
        ]
    sem = pltpu.SemaphoreType.DMA
    shapes = {
        "small": (5,), "w": (W_PARTS,), "own": (n,), "xs": (n, 2), "xr": (n, 2),
        "hs": (n,), "hr": (n, SECS - 1), "oss": (n, SECS - 1, 2), "orr": (n, 2), "osl": (n, 2),
        "s1s": (n,), "s1r": (n,), "ys": (n,), "yr": (n,), "s2s": (n,), "s2r": (n,),
        "bs": (n, 2), "br": (n, 2), "gs": (n, SECS - 1), "gr": (n,),
    }
    scratch += [sem(shape) for shape in shapes.values()]
    vmem = pl.BlockSpec(memory_space=pltpu.VMEM)
    anywhere = pl.BlockSpec(memory_space=pl.ANY)
    return pl.pallas_call(
        kernel,
        out_shape=jax.ShapeDtypeStruct((1, TILES, WIDE), f32),
        in_specs=[anywhere] * 6,
        out_specs=vmem,
        scratch_shapes=scratch,
        compiler_params=pltpu.CompilerParams(
            collective_id=0, has_side_effects=True, vmem_limit_bytes=56 * 2**20
        ),
    )(
        surface,
        weights,
        src_tiles.T,
        block_count[None],
        land_sea,
        exchange_coef[None],
    )


def solution(mesh):
    placed = (
        P("sec", "tile", None),
        P("tile", None, None),
        P("tile", None),
        P("tile"),
        P("tile", None),
        P(),
    )
    return jax.shard_map(
        on_device, mesh=mesh, in_specs=placed, out_specs=P("sec", "tile", None), check_vma=False
    )
```

```python
import functools
import jax
import jax.numpy as jnp
from jax import lax
from jax.experimental import pallas as pl
from jax.experimental.pallas import tpu as pltpu
from jax.sharding import PartitionSpec as P

MESH = pl.DeviceIdType.MESH
FIELDS, CELLS, BLOCKS, TILES = 40, 64, 8, 64
WIDE = FIELDS * CELLS
BANDS, SECS = 64, 4
KEEP = 48
GIVE = TILES - KEEP
SLOTS = 3 * KEEP
PAIRS = TILES // 2
HALF = PAIRS // 2
STEPS = 2
STEP = HALF // STEPS
CHUNKS = (16, 24)
W_PARTS = 8
RING = 4
f32, bf16 = jnp.float32, jnp.bfloat16


def split(x):
    hi = x.astype(bf16).astype(f32)
    return hi, x - hi


def kernel(x_ref, w_ref, ids_ref, used_ref, land_ref, coef_ref, out_ref, *scratch):
    n = len(CHUNKS)
    (wraw, wp, mix, hot, cb, fac, rel) = scratch[:7]
    (ids, used, land, coef_in, index, idx, wet, coef) = scratch[7:15]
    per = scratch[15 : 15 + 12 * n]
    (small, w_sem, own_sem, xs, xr, hs, hr, oss, orr, osl, s1s, s1r, ys, yr, s2s, s2r, bs, br, gs, gr) = (
        scratch[15 + 12 * n :]
    )
    band_in, part, sib, ysum, yrec, flux, oc, ocd, tot, rec, src, given = [
        [per[12 * i + j] for i in range(n)] for j in range(12)
    ]
    s, b = lax.axis_index("sec"), lax.axis_index("tile")
    core = lax.rem(s, 2)
    mate = s + 1 - 2 * core
    opp = lax.rem(s + 2, SECS)
    east, west = lax.rem(b + 1, BANDS), lax.rem(b + BANDS - 1, BANDS)
    taker = s == SECS - 1
    x = lax.rem(b, RING)
    east_sec = jnp.where(x == RING - 1, opp, s)
    west_sec = jnp.where(x == 0, opp, s)
    lane = lax.broadcasted_iota(jnp.int32, (1, 128), 1)
    low = lane < CELLS
    starts = [sum(CHUNKS[:i]) for i in range(n)]

    def remote(a, z, ss, rs, to):
        return pltpu.make_async_remote_copy(
            src_ref=a, dst_ref=z, send_sem=ss, recv_sem=rs, device_id=to, device_id_type=MESH
        )

    def lanes(i):
        return pl.ds(starts[i] * CELLS, CHUNKS[i] * CELLS)

    per_w = TILES // W_PARTS
    w_copy = [
        pltpu.make_async_copy(
            w_ref.at[pl.ds(i * per_w, per_w)], wraw.at[pl.ds(i * per_w, per_w)], w_sem.at[i]
        )
        for i in range(W_PARTS)
    ]
    keep_rows, give_rows = pl.ds(0, KEEP), pl.ds(KEEP, GIVE)
    own_copy = [
        pltpu.make_async_copy(x_ref.at[0, keep_rows, lanes(i)], band_in[i].at[1], own_sem.at[i])
        for i in range(n)
    ]

    def to_neighbours(i, block):
        return (
            remote(block, band_in[i].at[0], xs.at[i, 0], xr.at[i, 0], (east_sec, east)),
            remote(block, band_in[i].at[2], xs.at[i, 1], xr.at[i, 1], (west_sec, west)),
        )

    def hand_over(i, who):
        return remote(
            x_ref.at[0, give_rows, lanes(i)],
            band_in[i].at[1, pl.ds(pl.multiple_of(who * GIVE, GIVE), GIVE)],
            hs.at[i],
            hr.at[i, who],
            (SECS - 1, b),
        )

    def ocean_to(i, who, z):
        return remote(
            x_ref.at[0, pl.ds((who % 2) * HALF + z * PAIRS, HALF), lanes(i)],
            oc[i].at[pl.ds(z * HALF, HALF)],
            oss.at[i, who, z],
            orr.at[i, z],
            (who, b),
        )

    def ocean_own(i, z):
        return pltpu.make_async_copy(
            x_ref.at[0, pl.ds(HALF + z * PAIRS, HALF), lanes(i)],
            oc[i].at[pl.ds(z * HALF, HALF)],
            osl.at[i, z],
        )

    tables = [
        pltpu.make_async_copy(a, z, small.at[j])
        for j, (a, z) in enumerate(
            ((ids_ref, ids), (used_ref, used), (land_ref, land), (coef_ref, coef_in))
        )
    ]

    barrier = pltpu.get_barrier_semaphore()
    for q in (1, 2, 3):
        pl.semaphore_signal(
            barrier, inc=1, device_id=(lax.rem(s + q, SECS), b), device_id_type=MESH
        )
    for z in (east, west):
        for q in range(SECS):
            pl.semaphore_signal(
                barrier, inc=1, device_id=(lax.rem(s + q, SECS), z), device_id_type=MESH
            )
    for c in tables:
        c.start()
    for c in w_copy:
        c.start()

    @pl.when(jnp.logical_not(taker))
    def _():
        for i in range(n):
            own_copy[i].start()

    @pl.when(taker)
    def _():
        for i in range(n):
            for z in range(2):
                ocean_own(i, z).start()

    pl.semaphore_wait(barrier, 3 * SECS - 1)

    @pl.when(jnp.logical_not(taker))
    def _():
        for i in range(n):
            hand_over(i, s).start()
        for i in range(n):
            for c in to_neighbours(i, x_ref.at[0, keep_rows, lanes(i)]):
                c.start()

    def take_over(i):
        @pl.when(taker)
        def _():
            for who in range(SECS - 1):
                hand_over(i, who).wait_recv()
            for c in to_neighbours(i, band_in[i].at[1]):
                c.start()

    def prepare(t, _):
        for k in range(BLOCKS):
            hi, lo = split(wraw[t, pl.ds(k, CELLS // 2, stride=BLOCKS), :])
            left = jnp.where(low, hi, pltpu.roll(lo, CELLS, 1))
            right = jnp.where(low, pltpu.roll(hi, CELLS, 1), lo)
            mix[k, pl.ds(0, CELLS // 2, stride=2), :] = left
            mix[k, pl.ds(1, CELLS // 2, stride=2), :] = right
        for k in range(BLOCKS):
            wp[t, pl.ds(k * CELLS, CELLS), :] = mix[k].astype(bf16)
        return 0

    def prepare_part(i):
        w_copy[i].wait()
        lax.fori_loop(i * per_w, (i + 1) * per_w, prepare, 0, unroll=4)

    take_over(0)

    @pl.when(taker)
    def _():
        for i in range(n):
            for who in range(SECS - 1):
                for z in range(2):
                    ocean_to(i, who, z).start()

    for c in tables:
        c.wait()
    sec_tiles = BANDS * TILES
    source = ids[...] // sec_tiles
    within = ids[...] % sec_tiles
    slot = (within // TILES - b + 1 + BANDS) % BANDS
    row = within % TILES
    kept = row < KEEP
    owner = jnp.where(kept, source, SECS - 1)
    local = jnp.where(kept, row, source * GIVE + row - KEEP)
    holder = jnp.where(slot == 0, west_sec, jnp.where(slot == 2, east_sec, s))
    valid = lax.broadcasted_iota(jnp.int32, (BLOCKS, TILES), 0) < used[...]
    named = jnp.where(valid & (owner == holder), slot * KEEP + local, SLOTS)
    index[...] = jnp.concatenate([named, named], axis=1)
    to_smem = pltpu.make_async_copy(index, idx, small.at[len(tables)])
    to_smem.start()
    rows = lax.broadcasted_iota(jnp.int32, (SLOTS, 128), 0)
    for kpar in range(2):
        for h in range(2):
            k = 4 * h + kpar
            named = jnp.where(low, index[pl.ds(k, 1), :], index[pl.ds(k + 2, 1), :])
            at = pl.ds(128 * (2 * kpar + h), 128)
            hot[:, at] = jnp.where(rows == named, 1.0, 0.0).astype(bf16)
    dry = land[...].astype(f32)
    wet[...] = jnp.concatenate([dry[:PAIRS], dry[PAIRS:]], axis=1)
    square = [lax.broadcasted_iota(jnp.int32, (FIELDS, FIELDS), d) for d in range(2)]
    diagonal = jnp.where(square[0] == square[1], coef_in[...], 0.0)
    coef[...] = jnp.broadcast_to(jnp.sum(diagonal, axis=1, keepdims=True), (FIELDS, 128))

    for i in range(W_PARTS):
        prepare_part(i)
        if i + 1 < n:
            take_over(i + 1)
    to_smem.wait()

    def spread(view, count, F, dst, base):
        for g in range(count // 8):
            for j in range(F // 2):
                v = view[pl.ds(8 * g, 8), pl.ds(128 * j, 128)]
                r = pltpu.roll(v, CELLS, 1)
                at = (base + 8 * g) * F + 2 * j
                dst[pl.ds(at, 8, stride=F), :] = jnp.where(low, v, r)
                dst[pl.ds(at + 1, 8, stride=F), :] = jnp.where(low, r, v)

    def forward(i):
        F = CHUNKS[i]

        @pl.when(jnp.logical_not(taker))
        def _():
            own_copy[i].wait()

        src[i][SLOTS] = jnp.zeros((F, 128), f32)
        flat = src[i].reshape((SLOTS + 1) * F, 128)
        spread(band_in[i].at[1], KEEP, F, flat, KEEP)
        arrivals = to_neighbours(i, band_in[i].at[1])
        arrivals[0].wait_recv()
        spread(band_in[i].at[0], KEEP, F, flat, 0)
        arrivals[1].wait_recv()
        spread(band_in[i].at[2], KEEP, F, flat, 2 * KEEP)

        def pair(p, _):
            q = []
            for tp in range(2):
                t = p + PAIRS * tp
                cols = []
                for kp in range(BLOCKS // 2):
                    g0 = idx[2 * kp, t]
                    g1 = idx[2 * kp + 1, t]
                    cols.append(
                        jnp.where(
                            low,
                            src[i][g0],
                            src[i][g1],
                        )
                    )
                hi, lo = split(jnp.concatenate(cols, axis=1))
                lhs = jnp.concatenate([hi, lo], axis=0).astype(bf16)
                o = jnp.dot(lhs, wp[t], preferred_element_type=f32)
                q.append(o[:F] + pltpu.roll(o[:F], CELLS, 1) + o[F:])
            part[i][pl.ds(pl.multiple_of(p * F, 8), F), :] = jnp.where(
                low, q[0], pltpu.roll(q[1], CELLS, 1)
            )
            return 0

        def other(q, _):
            lax.fori_loop(
                0, STEP, lambda u, c: pair((1 - core) * HALF + q * STEP + u, c), 0, unroll=STEP
            )
            sib_copy(i, q).start()
            return 0

        def own(q, _):
            lax.fori_loop(
                0, STEP, lambda u, c: pair(core * HALF + q * STEP + u, c), 0, unroll=STEP
            )
            at = step_rows(i, q)
            sib_copy(i, q).wait_recv()
            ysum[i][at, :] = part[i][half_rows(i, core, q), :] + sib[i][at, :]
            y_copy(i, q).start()
            return 0

        lax.fori_loop(0, STEPS, other, 0)
        lax.fori_loop(0, STEPS, own, 0)

    def step_rows(i, q):
        size = STEP * CHUNKS[i]
        return pl.ds(pl.multiple_of(q * size, 8), size)

    def half_rows(i, which, q):
        size = STEP * CHUNKS[i]
        return pl.ds(pl.multiple_of((which * STEPS + q) * size, 8), size)

    def sib_copy(i, q):
        return remote(
            part[i].at[half_rows(i, 1 - core, q)],
            sib[i].at[step_rows(i, q)],
            s1s.at[i, q],
            s1r.at[i, q],
            (mate, b),
        )

    def y_copy(i, q):
        at = step_rows(i, q)
        return remote(ysum[i].at[at], yrec[i].at[at], ys.at[i, q], yr.at[i, q], (opp, b))

    def flux_copy(i, which, q):
        at = flux[i].at[half_rows(i, which, q)]
        return remote(at, at, s2s.at[i, q], s2r.at[i, q], (mate, b))

    def prepare_ocean(i):
        @pl.when(taker)
        def _():
            for z in range(2):
                ocean_own(i, z).wait()

        @pl.when(jnp.logical_not(taker))
        def _():
            for z in range(2):
                ocean_to(i, 0, z).wait_recv()

        spread(oc[i], 2 * HALF, CHUNKS[i], ocd[i], 0)

    def fluxes(i, q):
        F = CHUNKS[i]
        y_copy(i, q).wait_recv()
        for v in range(STEP):
            u = q * STEP + v
            at = pl.ds(pl.multiple_of(u * F, 8), F)
            a = ocd[i][at, :]
            z = ocd[i][pl.ds(pl.multiple_of((HALF + u) * F, 8), F), :]
            rel[at, :] = ysum[i][at, :] + yrec[i][at, :] - jnp.where(low, a, z)
        here = pl.ds(pl.multiple_of(q * STEP, 8), STEP)
        if i == 0:
            r0, r1, r2 = [rel[pl.ds(q * STEP * F + f, STEP, stride=F), :] for f in range(3)]
            speed = jnp.sqrt(r0 * r0 + r1 * r1 + 0.25)
            stab = 1.0 + 0.5 * jnp.tanh(-r2)
            sea = wet[pl.ds(pl.multiple_of(core * HALF + q * STEP, 8), STEP), :]
            fac[here, :] = speed * stab * sea
        exchange = coef[pl.ds(starts[i], F), :]
        for v in range(STEP):
            u = q * STEP + v
            at = pl.ds(pl.multiple_of(u * F, 8), F)
            to = pl.ds(pl.multiple_of((core * HALF + u) * F, 8), F)
            flux[i][to, :] = exchange * fac[pl.ds(u, 1), :] * rel[at, :]
        flux_copy(i, core, q).start()

    def backward(i):
        F = CHUNKS[i]

        def pair(p, _):
            v = flux[i][pl.ds(pl.multiple_of(p * F, 8), F), :]
            r = pltpu.roll(v, CELLS, 1)
            for tp in range(2):
                t = p + PAIRS * tp
                hi, lo = split(jnp.where(low, v, r) if tp == 0 else jnp.where(low, r, v))
                lhs = jnp.concatenate([hi, lo], axis=0).astype(bf16)
                o = lax.dot_general(
                    lhs, wp[t], (((1,), (1,)), ((), ())), preferred_element_type=f32
                )
                o = o[:F] + o[F:]
                for kp in range(BLOCKS // 2):
                    at = pl.multiple_of((kp * TILES + t) * F, 8)
                    cb[pl.ds(at, F), :] = o[:, 128 * kp : 128 * kp + 128]
            return 0

        def own(q, _):
            fluxes(i, q)
            lax.fori_loop(
                0, STEP, lambda u, c: pair(core * HALF + q * STEP + u, c), 0, unroll=STEP
            )
            return 0

        def other(q, _):
            flux_copy(i, 1 - core, q).wait_recv()
            lax.fori_loop(
                0, STEP, lambda u, c: pair((1 - core) * HALF + q * STEP + u, c), 0, unroll=STEP
            )
            return 0

        lax.fori_loop(0, STEPS, own, 0)
        lax.fori_loop(0, STEPS, other, 0)

        def gather(j, _):
            count = TILES * BLOCKS // 2
            x0 = cb[pl.ds(2 * j, count, stride=F), :]
            x1 = cb[pl.ds(2 * j + 1, count, stride=F), :]
            top = jnp.where(low, x0, pltpu.roll(x1, CELLS, 1))
            bottom = jnp.where(low, pltpu.roll(x0, CELLS, 1), x1)
            hi, lo = split(jnp.concatenate([top, bottom], axis=0))
            rhs = jnp.concatenate([hi, lo], axis=1).astype(bf16)
            o = jnp.dot(hot[...], rhs, preferred_element_type=f32)
            o = o[:, :128] + o[:, 128:]
            at = pl.ds(pl.multiple_of(128 * j, 128), 128)
            for z in range(3):
                tot[i][z, :, at] = o[z * KEEP : (z + 1) * KEEP]
            return 0

        for g in range(2):
            lax.fori_loop(g * F // 4, (g + 1) * F // 4, gather, 0, unroll=F // 4)
            for when, c in back_copies(i, g):
                pl.when(when)(c.start)

    def back_copies(i, g):
        size = CHUNKS[i] * CELLS // 2
        at = pl.ds(g * size, size)
        copies = []
        for o, sec, to in ((0, west_sec, west), (2, east_sec, east), (1, s, b)):
            if o != 1:
                z = (2 - o) // 2
                c = remote(
                    tot[i].at[o, :, at],
                    rec[i].at[z, :, at],
                    bs.at[i, g, o],
                    br.at[i, g, z],
                    (sec, to),
                )
                copies.append((sec != SECS - 1, c))
            for who in range(SECS - 1):
                c = remote(
                    tot[i].at[o, pl.ds(GIVE * who, GIVE), at],
                    given[i].at[2 - o, :, at],
                    gs.at[i, g, o, who],
                    gr.at[i, g, 2 - o],
                    (who, to),
                )
                copies.append((sec == SECS - 1, c))
        return copies

    def back_arrivals(i, g):
        size = CHUNKS[i] * CELLS // 2
        at = pl.ds(g * size, size)
        copies = []
        for z in range(2):
            block = rec[i].at[z, :, at]
            copies.append(remote(block, block, bs.at[i, g, 0], br.at[i, g, z], (opp, b)))
        for z in range(3):
            block = given[i].at[z, :, at]
            copies.append(remote(block, block, bs.at[i, g, 0], gr.at[i, g, z], (opp, b)))
        return copies

    def ocean_out(i):
        F = CHUNKS[i]
        for g in range(PAIRS // 8):
            for j in range(F // 2):
                x0 = flux[i][pl.ds(8 * g * F + 2 * j, 8, stride=F), :]
                x1 = flux[i][pl.ds(8 * g * F + 2 * j + 1, 8, stride=F), :]
                at = pl.ds(starts[i] * CELLS + 128 * j, 128)
                out_ref[0, pl.ds(8 * g, 8), at] = jnp.where(low, x0, pltpu.roll(x1, CELLS, 1))
                out_ref[0, pl.ds(PAIRS + 8 * g, 8), at] = jnp.where(
                    low, pltpu.roll(x0, CELLS, 1), x1
                )

    def finish(i):
        for g in range(2):
            for c in back_arrivals(i, g):
                c.wait_recv()
        out_ref[0, keep_rows, lanes(i)] = tot[i][1] + rec[i][0] + rec[i][1]
        out_ref[0, give_rows, lanes(i)] = given[i][0] + given[i][1] + given[i][2]

    for i in range(n):
        forward(i)
        prepare_ocean(i)
    for i in range(n):
        backward(i)

    @pl.when(taker)
    def _():
        for i in range(n):
            ocean_out(i)

    @pl.when(jnp.logical_not(taker))
    def _():
        for i in range(n):
            finish(i)

    for i in range(n):
        for c in to_neighbours(i, band_in[i].at[1]):
            c.wait_send()
        for q in range(STEPS):
            sib_copy(i, q).wait_send()
            y_copy(i, q).wait_send()
            flux_copy(i, core, q).wait_send()
        for g in range(2):
            for when, c in back_copies(i, g):
                pl.when(when)(c.wait_send)

    @pl.when(taker)
    def _():
        for i in range(n):
            for who in range(SECS - 1):
                for z in range(2):
                    ocean_to(i, who, z).wait_send()

    @pl.when(jnp.logical_not(taker))
    def _():
        for i in range(n):
            hand_over(i, s).wait_send()


def on_device(surface, remap_weights, src_tiles, block_count, land_sea, exchange_coef):
    n = len(CHUNKS)
    weights = (
        remap_weights.reshape(TILES, BLOCKS, CELLS // 2, 128)
        .transpose(0, 2, 1, 3)
        .reshape(TILES, BLOCKS * CELLS // 2, 128)
    )
    top = max(CHUNKS)
    scratch = [
        pltpu.VMEM((TILES, BLOCKS * CELLS // 2, 128), f32),
        pltpu.VMEM((TILES, BLOCKS * CELLS, 128), bf16),
        pltpu.VMEM((BLOCKS, CELLS, 128), f32),
        pltpu.VMEM((SLOTS, TILES * BLOCKS), bf16),
        pltpu.VMEM((TILES * BLOCKS // 2 * top, 128), f32),
        pltpu.VMEM((HALF, 128), f32),
        pltpu.VMEM((HALF * top, 128), f32),
        pltpu.VMEM((BLOCKS, TILES), jnp.int32),
        pltpu.VMEM((1, TILES), jnp.int32),
        pltpu.VMEM((TILES, CELLS), jnp.int32),
        pltpu.VMEM((1, FIELDS), f32),
        pltpu.VMEM((BLOCKS, 128), jnp.int32),
        pltpu.SMEM((BLOCKS, 128), jnp.int32),
        pltpu.VMEM((PAIRS, 128), f32),
        pltpu.VMEM((FIELDS, 128), f32),
    ]
    for F in CHUNKS:
        scratch += [
            pltpu.VMEM((3, KEEP, F * CELLS), f32),
            pltpu.VMEM((PAIRS * F, 128), f32),
            pltpu.VMEM((HALF * F, 128), f32),
            pltpu.VMEM((HALF * F, 128), f32),
            pltpu.VMEM((HALF * F, 128), f32),
            pltpu.VMEM((PAIRS * F, 128), f32),
            pltpu.VMEM((2 * HALF, F * CELLS), f32),
            pltpu.VMEM((2 * HALF * F, 128), f32),
            pltpu.VMEM((3, KEEP, F * CELLS), f32),
            pltpu.VMEM((2, KEEP, F * CELLS), f32),
            pltpu.VMEM((SLOTS + 1, F, 128), f32),
            pltpu.VMEM((3, GIVE, F * CELLS), f32),
        ]
    sem = pltpu.SemaphoreType.DMA
    shapes = {
        "small": (5,), "w": (W_PARTS,), "own": (n,), "xs": (n, 2), "xr": (n, 2),
        "hs": (n,), "hr": (n, SECS - 1), "oss": (n, SECS - 1, 2), "orr": (n, 2), "osl": (n, 2),
        "s1s": (n, STEPS), "s1r": (n, STEPS), "ys": (n, STEPS), "yr": (n, STEPS),
        "s2s": (n, STEPS), "s2r": (n, STEPS), "bs": (n, 2, 3), "br": (n, 2, 2),
        "gs": (n, 2, 3, SECS - 1), "gr": (n, 2, 3),
    }
    scratch += [sem(shape) for shape in shapes.values()]
    vmem = pl.BlockSpec(memory_space=pltpu.VMEM)
    anywhere = pl.BlockSpec(memory_space=pl.ANY)
    return pl.pallas_call(
        kernel,
        out_shape=jax.ShapeDtypeStruct((1, TILES, WIDE), f32),
        in_specs=[anywhere] * 6,
        out_specs=vmem,
        scratch_shapes=scratch,
        compiler_params=pltpu.CompilerParams(
            collective_id=0, has_side_effects=True, vmem_limit_bytes=56 * 2**20
        ),
    )(
        surface,
        weights,
        src_tiles.T,
        block_count[None],
        land_sea,
        exchange_coef[None],
    )


def solution(mesh):
    placed = (
        P("sec", "tile", None),
        P("tile", None, None),
        P("tile", None),
        P("tile"),
        P("tile", None),
        P(),
    )
    return jax.shard_map(
        on_device, mesh=mesh, in_specs=placed, out_specs=P("sec", "tile", None), check_vma=False
    )
```

```python
import functools
import jax
import jax.numpy as jnp
from jax import lax
from jax.experimental import pallas as pl
from jax.experimental.pallas import tpu as pltpu
from jax.sharding import PartitionSpec as P

MESH = pl.DeviceIdType.MESH
FIELDS, CELLS, BLOCKS, TILES = 40, 64, 8, 64
WIDE = FIELDS * CELLS
BANDS, SECS = 64, 4
KEEP = 48
GIVE = TILES - KEEP
SLOTS = 3 * KEEP
PAIRS = TILES // 2
HALF = PAIRS // 2
STEPS = 2
STEP = HALF // STEPS
CHUNKS = (16, 24)
W_PARTS = 8
RING = 4
f32, bf16 = jnp.float32, jnp.bfloat16


def split(x):
    hi = x.astype(bf16).astype(f32)
    return hi, x - hi


def kernel(x_ref, w_ref, ids_ref, used_ref, land_ref, coef_ref, out_ref, *scratch):
    n = len(CHUNKS)
    (wraw, wp, mix, hot, cb, fac, rel, res) = scratch[:8]
    (ids, used, land, coef_in, index, idx, wet, coef) = scratch[8:16]
    per = scratch[16 : 16 + 12 * n]
    (small, out_sem, w_sem, own_sem, xs, xr, hs, hr, oss, orr, osl, s1s, s1r, ys, yr, s2s, s2r, bs, br, gs, gr) = (
        scratch[16 + 12 * n :]
    )
    band_in, part, sib, ysum, yrec, flux, oc, ocd, tot, rec, src, given = [
        [per[12 * i + j] for i in range(n)] for j in range(12)
    ]
    s, b = lax.axis_index("sec"), lax.axis_index("tile")
    core = lax.rem(s, 2)
    mate = s + 1 - 2 * core
    opp = lax.rem(s + 2, SECS)
    east, west = lax.rem(b + 1, BANDS), lax.rem(b + BANDS - 1, BANDS)
    taker = s == SECS - 1
    x = lax.rem(b, RING)
    east_sec = jnp.where(x == RING - 1, opp, s)
    west_sec = jnp.where(x == 0, opp, s)
    lane = lax.broadcasted_iota(jnp.int32, (1, 128), 1)
    low = lane < CELLS
    starts = [sum(CHUNKS[:i]) for i in range(n)]

    def remote(a, z, ss, rs, to):
        return pltpu.make_async_remote_copy(
            src_ref=a, dst_ref=z, send_sem=ss, recv_sem=rs, device_id=to, device_id_type=MESH
        )

    def lanes(i):
        return pl.ds(starts[i] * CELLS, CHUNKS[i] * CELLS)

    per_w = TILES // W_PARTS
    w_copy = [
        pltpu.make_async_copy(
            w_ref.at[pl.ds(i * per_w, per_w)], wraw.at[pl.ds(i * per_w, per_w)], w_sem.at[i]
        )
        for i in range(W_PARTS)
    ]
    keep_rows, give_rows = pl.ds(0, KEEP), pl.ds(KEEP, GIVE)
    own_copy = [
        pltpu.make_async_copy(x_ref.at[0, keep_rows, lanes(i)], band_in[i].at[1], own_sem.at[i])
        for i in range(n)
    ]

    def to_neighbours(i, block):
        return (
            remote(block, band_in[i].at[0], xs.at[i, 0], xr.at[i, 0], (east_sec, east)),
            remote(block, band_in[i].at[2], xs.at[i, 1], xr.at[i, 1], (west_sec, west)),
        )

    def hand_over(i, who):
        return remote(
            x_ref.at[0, give_rows, lanes(i)],
            band_in[i].at[1, pl.ds(pl.multiple_of(who * GIVE, GIVE), GIVE)],
            hs.at[i],
            hr.at[i, who],
            (SECS - 1, b),
        )

    def ocean_to(i, who, z):
        return remote(
            x_ref.at[0, pl.ds((who % 2) * HALF + z * PAIRS, HALF), lanes(i)],
            oc[i].at[pl.ds(z * HALF, HALF)],
            oss.at[i, who, z],
            orr.at[i, z],
            (who, b),
        )

    def ocean_own(i, z):
        return pltpu.make_async_copy(
            x_ref.at[0, pl.ds(HALF + z * PAIRS, HALF), lanes(i)],
            oc[i].at[pl.ds(z * HALF, HALF)],
            osl.at[i, z],
        )

    tables = [
        pltpu.make_async_copy(a, z, small.at[j])
        for j, (a, z) in enumerate(
            ((ids_ref, ids), (used_ref, used), (land_ref, land), (coef_ref, coef_in))
        )
    ]

    barrier = pltpu.get_barrier_semaphore()
    for q in (1, 2, 3):
        pl.semaphore_signal(
            barrier, inc=1, device_id=(lax.rem(s + q, SECS), b), device_id_type=MESH
        )
    for z in (east, west):
        for q in range(SECS):
            pl.semaphore_signal(
                barrier, inc=1, device_id=(lax.rem(s + q, SECS), z), device_id_type=MESH
            )
    for c in tables:
        c.start()
    for c in w_copy:
        c.start()

    @pl.when(jnp.logical_not(taker))
    def _():
        for i in range(n):
            own_copy[i].start()

    @pl.when(taker)
    def _():
        for i in range(n):
            for z in range(2):
                ocean_own(i, z).start()

    pl.semaphore_wait(barrier, 3 * SECS - 1)

    @pl.when(jnp.logical_not(taker))
    def _():
        for i in range(n):
            hand_over(i, s).start()
        for i in range(n):
            for c in to_neighbours(i, x_ref.at[0, keep_rows, lanes(i)]):
                c.start()

    def take_over(i):
        @pl.when(taker)
        def _():
            for who in range(SECS - 1):
                hand_over(i, who).wait_recv()
            for c in to_neighbours(i, band_in[i].at[1]):
                c.start()

    def prepare(t, _):
        for k in range(BLOCKS):
            hi, lo = split(wraw[t, pl.ds(k, CELLS // 2, stride=BLOCKS), :])
            left = jnp.where(low, hi, pltpu.roll(lo, CELLS, 1))
            right = jnp.where(low, pltpu.roll(hi, CELLS, 1), lo)
            mix[k, pl.ds(0, CELLS // 2, stride=2), :] = left
            mix[k, pl.ds(1, CELLS // 2, stride=2), :] = right
        for k in range(BLOCKS):
            wp[t, pl.ds(k * CELLS, CELLS), :] = mix[k].astype(bf16)
        return 0

    def prepare_part(i):
        w_copy[i].wait()
        lax.fori_loop(i * per_w, (i + 1) * per_w, prepare, 0, unroll=4)

    take_over(0)

    @pl.when(taker)
    def _():
        for i in range(n):
            for who in range(SECS - 1):
                for z in range(2):
                    ocean_to(i, who, z).start()

    for c in tables:
        c.wait()
    sec_tiles = BANDS * TILES
    source = ids[...] // sec_tiles
    within = ids[...] % sec_tiles
    slot = (within // TILES - b + 1 + BANDS) % BANDS
    row = within % TILES
    kept = row < KEEP
    owner = jnp.where(kept, source, SECS - 1)
    local = jnp.where(kept, row, source * GIVE + row - KEEP)
    holder = jnp.where(slot == 0, west_sec, jnp.where(slot == 2, east_sec, s))
    valid = lax.broadcasted_iota(jnp.int32, (BLOCKS, TILES), 0) < used[...]
    named = jnp.where(valid & (owner == holder), slot * KEEP + local, SLOTS)
    index[...] = jnp.concatenate([named, named], axis=1)
    to_smem = pltpu.make_async_copy(index, idx, small.at[len(tables)])
    to_smem.start()
    rows = lax.broadcasted_iota(jnp.int32, (SLOTS, 128), 0)
    for kpar in range(2):
        for h in range(2):
            k = 4 * h + kpar
            named = jnp.where(low, index[pl.ds(k, 1), :], index[pl.ds(k + 2, 1), :])
            at = pl.ds(128 * (2 * kpar + h), 128)
            hot[:, at] = jnp.where(rows == named, 1.0, 0.0).astype(bf16)
    dry = land[...].astype(f32)
    wet[...] = jnp.concatenate([dry[:PAIRS], dry[PAIRS:]], axis=1)
    square = [lax.broadcasted_iota(jnp.int32, (FIELDS, FIELDS), d) for d in range(2)]
    diagonal = jnp.where(square[0] == square[1], coef_in[...], 0.0)
    coef[...] = jnp.broadcast_to(jnp.sum(diagonal, axis=1, keepdims=True), (FIELDS, 128))

    for i in range(W_PARTS):
        prepare_part(i)
        if i + 1 < n:
            take_over(i + 1)
    to_smem.wait()

    def spread(view, count, F, dst, base):
        for g in range(count // 8):
            for j in range(F // 2):
                v = view[pl.ds(8 * g, 8), pl.ds(128 * j, 128)]
                r = pltpu.roll(v, CELLS, 1)
                at = (base + 8 * g) * F + 2 * j
                dst[pl.ds(at, 8, stride=F), :] = jnp.where(low, v, r)
                dst[pl.ds(at + 1, 8, stride=F), :] = jnp.where(low, r, v)

    def forward(i):
        F = CHUNKS[i]

        @pl.when(jnp.logical_not(taker))
        def _():
            own_copy[i].wait()

        src[i][SLOTS] = jnp.zeros((F, 128), f32)
        flat = src[i].reshape((SLOTS + 1) * F, 128)
        spread(band_in[i].at[1], KEEP, F, flat, KEEP)
        if i + 1 == n:
            for later in range(1, n):
                prepare_ocean(later)
        arrivals = to_neighbours(i, band_in[i].at[1])
        arrivals[0].wait_recv()
        spread(band_in[i].at[0], KEEP, F, flat, 0)
        arrivals[1].wait_recv()
        spread(band_in[i].at[2], KEEP, F, flat, 2 * KEEP)

        def pair(p, _):
            q = []
            for tp in range(2):
                t = p + PAIRS * tp
                cols = []
                for kp in range(BLOCKS // 2):
                    g0 = idx[2 * kp, t]
                    g1 = idx[2 * kp + 1, t]
                    cols.append(
                        jnp.where(
                            low,
                            src[i][g0],
                            src[i][g1],
                        )
                    )
                hi, lo = split(jnp.concatenate(cols, axis=1))
                lhs = jnp.concatenate([hi, lo], axis=0).astype(bf16)
                o = jnp.dot(lhs, wp[t], preferred_element_type=f32)
                q.append(o[:F] + pltpu.roll(o[:F], CELLS, 1) + o[F:])
            part[i][pl.ds(pl.multiple_of(p * F, 8), F), :] = jnp.where(
                low, q[0], pltpu.roll(q[1], CELLS, 1)
            )
            return 0

        def other(q, _):
            lax.fori_loop(
                0, STEP, lambda u, c: pair((1 - core) * HALF + q * STEP + u, c), 0, unroll=STEP
            )
            sib_copy(i, q).start()
            return 0

        def own(q, _):
            lax.fori_loop(
                0, STEP, lambda u, c: pair(core * HALF + q * STEP + u, c), 0, unroll=STEP
            )
            at = step_rows(i, q)
            sib_copy(i, q).wait_recv()
            ysum[i][at, :] = part[i][half_rows(i, core, q), :] + sib[i][at, :]
            y_copy(i, q).start()
            return 0

        lax.fori_loop(0, STEPS, other, 0)
        lax.fori_loop(0, STEPS, own, 0)

    def step_rows(i, q):
        size = STEP * CHUNKS[i]
        return pl.ds(pl.multiple_of(q * size, 8), size)

    def half_rows(i, which, q):
        size = STEP * CHUNKS[i]
        return pl.ds(pl.multiple_of((which * STEPS + q) * size, 8), size)

    def sib_copy(i, q):
        return remote(
            part[i].at[half_rows(i, 1 - core, q)],
            sib[i].at[step_rows(i, q)],
            s1s.at[i, q],
            s1r.at[i, q],
            (mate, b),
        )

    def y_copy(i, q):
        at = step_rows(i, q)
        return remote(ysum[i].at[at], yrec[i].at[at], ys.at[i, q], yr.at[i, q], (opp, b))

    def flux_copy(i, which, q):
        at = flux[i].at[half_rows(i, which, q)]
        return remote(at, at, s2s.at[i, q], s2r.at[i, q], (mate, b))

    def prepare_ocean(i):
        @pl.when(taker)
        def _():
            for z in range(2):
                ocean_own(i, z).wait()

        @pl.when(jnp.logical_not(taker))
        def _():
            for z in range(2):
                ocean_to(i, 0, z).wait_recv()

        spread(oc[i], 2 * HALF, CHUNKS[i], ocd[i], 0)

    def fluxes(i, q):
        F = CHUNKS[i]
        y_copy(i, q).wait_recv()
        for v in range(STEP):
            u = q * STEP + v
            at = pl.ds(pl.multiple_of(u * F, 8), F)
            a = ocd[i][at, :]
            z = ocd[i][pl.ds(pl.multiple_of((HALF + u) * F, 8), F), :]
            rel[at, :] = ysum[i][at, :] + yrec[i][at, :] - jnp.where(low, a, z)
        here = pl.ds(pl.multiple_of(q * STEP, 8), STEP)
        if i == 0:
            r0, r1, r2 = [rel[pl.ds(q * STEP * F + f, STEP, stride=F), :] for f in range(3)]
            speed = jnp.sqrt(r0 * r0 + r1 * r1 + 0.25)
            stab = 1.0 + 0.5 * jnp.tanh(-r2)
            sea = wet[pl.ds(pl.multiple_of(core * HALF + q * STEP, 8), STEP), :]
            fac[here, :] = speed * stab * sea
        exchange = coef[pl.ds(starts[i], F), :]
        for v in range(STEP):
            u = q * STEP + v
            at = pl.ds(pl.multiple_of(u * F, 8), F)
            to = pl.ds(pl.multiple_of((core * HALF + u) * F, 8), F)
            flux[i][to, :] = exchange * fac[pl.ds(u, 1), :] * rel[at, :]
        flux_copy(i, core, q).start()

    def backward(i):
        F = CHUNKS[i]

        def pair(p, _):
            v = flux[i][pl.ds(pl.multiple_of(p * F, 8), F), :]
            r = pltpu.roll(v, CELLS, 1)
            for tp in range(2):
                t = p + PAIRS * tp
                hi, lo = split(jnp.where(low, v, r) if tp == 0 else jnp.where(low, r, v))
                lhs = jnp.concatenate([hi, lo], axis=0).astype(bf16)
                o = lax.dot_general(
                    lhs, wp[t], (((1,), (1,)), ((), ())), preferred_element_type=f32
                )
                o = o[:F] + o[F:]
                for kp in range(BLOCKS // 2):
                    at = pl.multiple_of((kp * TILES + t) * F, 8)
                    cb[pl.ds(at, F), :] = o[:, 128 * kp : 128 * kp + 128]
            return 0

        def own(q, _):
            fluxes(i, q)
            lax.fori_loop(
                0, STEP, lambda u, c: pair(core * HALF + q * STEP + u, c), 0, unroll=STEP
            )
            return 0

        def other(q, _):
            flux_copy(i, 1 - core, q).wait_recv()
            lax.fori_loop(
                0, STEP, lambda u, c: pair((1 - core) * HALF + q * STEP + u, c), 0, unroll=STEP
            )
            return 0

        lax.fori_loop(0, STEPS, own, 0)
        lax.fori_loop(0, STEPS, other, 0)

        def gather(j, _):
            count = TILES * BLOCKS // 2
            x0 = cb[pl.ds(2 * j, count, stride=F), :]
            x1 = cb[pl.ds(2 * j + 1, count, stride=F), :]
            top = jnp.where(low, x0, pltpu.roll(x1, CELLS, 1))
            bottom = jnp.where(low, pltpu.roll(x0, CELLS, 1), x1)
            hi, lo = split(jnp.concatenate([top, bottom], axis=0))
            rhs = jnp.concatenate([hi, lo], axis=1).astype(bf16)
            o = jnp.dot(hot[...], rhs, preferred_element_type=f32)
            o = o[:, :128] + o[:, 128:]
            at = pl.ds(pl.multiple_of(128 * j, 128), 128)
            for z in range(3):
                tot[i][z, :, at] = o[z * KEEP : (z + 1) * KEEP]
            return 0

        for g in range(2):
            lax.fori_loop(g * F // 4, (g + 1) * F // 4, gather, 0, unroll=F // 4)
            for when, c in back_copies(i, g):
                pl.when(when)(c.start)

    def back_copies(i, g):
        size = CHUNKS[i] * CELLS // 2
        at = pl.ds(g * size, size)
        copies = []
        for o, sec, to in ((0, west_sec, west), (2, east_sec, east), (1, s, b)):
            if o != 1:
                z = (2 - o) // 2
                c = remote(
                    tot[i].at[o, :, at],
                    rec[i].at[z, :, at],
                    bs.at[i, g, o],
                    br.at[i, g, z],
                    (sec, to),
                )
                copies.append((sec != SECS - 1, c))
            for who in range(SECS - 1):
                c = remote(
                    tot[i].at[o, pl.ds(GIVE * who, GIVE), at],
                    given[i].at[2 - o, :, at],
                    gs.at[i, g, o, who],
                    gr.at[i, g, 2 - o],
                    (who, to),
                )
                copies.append((sec == SECS - 1, c))
        return copies

    def back_arrivals(i, g):
        size = CHUNKS[i] * CELLS // 2
        at = pl.ds(g * size, size)
        copies = []
        for z in range(2):
            block = rec[i].at[z, :, at]
            copies.append(remote(block, block, bs.at[i, g, 0], br.at[i, g, z], (opp, b)))
        for z in range(3):
            block = given[i].at[z, :, at]
            copies.append(remote(block, block, bs.at[i, g, 0], gr.at[i, g, z], (opp, b)))
        return copies

    def ocean_out(i):
        F = CHUNKS[i]
        for g in range(PAIRS // 8):
            for j in range(F // 2):
                x0 = flux[i][pl.ds(8 * g * F + 2 * j, 8, stride=F), :]
                x1 = flux[i][pl.ds(8 * g * F + 2 * j + 1, 8, stride=F), :]
                at = pl.ds(starts[i] * CELLS + 128 * j, 128)
                res[pl.ds(8 * g, 8), at] = jnp.where(low, x0, pltpu.roll(x1, CELLS, 1))
                res[pl.ds(PAIRS + 8 * g, 8), at] = jnp.where(
                    low, pltpu.roll(x0, CELLS, 1), x1
                )

    def out_copy(i, g):
        size = CHUNKS[i] * CELLS // 2
        at = pl.ds(starts[i] * CELLS + g * size, size)
        return pltpu.make_async_copy(res.at[:, at], out_ref.at[0, :, at], out_sem.at[i, g])

    def finish(i, g):
        size = CHUNKS[i] * CELLS // 2
        at, to = pl.ds(g * size, size), pl.ds(starts[i] * CELLS + g * size, size)
        for c in back_arrivals(i, g):
            c.wait_recv()
        res[keep_rows, to] = tot[i][1, :, at] + rec[i][0, :, at] + rec[i][1, :, at]
        res[give_rows, to] = given[i][0, :, at] + given[i][1, :, at] + given[i][2, :, at]
        out_copy(i, g).start()

    for i in range(n):
        forward(i)
        if i == 0:
            prepare_ocean(i)
    for i in range(n):
        backward(i)

    @pl.when(taker)
    def _():
        for i in range(n):
            ocean_out(i)
            for g in range(2):
                out_copy(i, g).start()

    @pl.when(jnp.logical_not(taker))
    def _():
        for i in range(n):
            for g in range(2):
                finish(i, g)

    for i in range(n):
        for c in to_neighbours(i, band_in[i].at[1]):
            c.wait_send()
        for q in range(STEPS):
            sib_copy(i, q).wait_send()
            y_copy(i, q).wait_send()
            flux_copy(i, core, q).wait_send()
        for g in range(2):
            out_copy(i, g).wait()
            for when, c in back_copies(i, g):
                pl.when(when)(c.wait_send)

    @pl.when(taker)
    def _():
        for i in range(n):
            for who in range(SECS - 1):
                for z in range(2):
                    ocean_to(i, who, z).wait_send()

    @pl.when(jnp.logical_not(taker))
    def _():
        for i in range(n):
            hand_over(i, s).wait_send()


def on_device(surface, remap_weights, src_tiles, block_count, land_sea, exchange_coef):
    n = len(CHUNKS)
    weights = (
        remap_weights.reshape(TILES, BLOCKS, CELLS // 2, 128)
        .transpose(0, 2, 1, 3)
        .reshape(TILES, BLOCKS * CELLS // 2, 128)
    )
    top = max(CHUNKS)
    scratch = [
        pltpu.VMEM((TILES, BLOCKS * CELLS // 2, 128), f32),
        pltpu.VMEM((TILES, BLOCKS * CELLS, 128), bf16),
        pltpu.VMEM((BLOCKS, CELLS, 128), f32),
        pltpu.VMEM((SLOTS, TILES * BLOCKS), bf16),
        pltpu.VMEM((TILES * BLOCKS // 2 * top, 128), f32),
        pltpu.VMEM((HALF, 128), f32),
        pltpu.VMEM((HALF * top, 128), f32),
        pltpu.VMEM((TILES, WIDE), f32),
        pltpu.VMEM((BLOCKS, TILES), jnp.int32),
        pltpu.VMEM((1, TILES), jnp.int32),
        pltpu.VMEM((TILES, CELLS), jnp.int32),
        pltpu.VMEM((1, FIELDS), f32),
        pltpu.VMEM((BLOCKS, 128), jnp.int32),
        pltpu.SMEM((BLOCKS, 128), jnp.int32),
        pltpu.VMEM((PAIRS, 128), f32),
        pltpu.VMEM((FIELDS, 128), f32),
    ]
    for F in CHUNKS:
        scratch += [
            pltpu.VMEM((3, KEEP, F * CELLS), f32),
            pltpu.VMEM((PAIRS * F, 128), f32),
            pltpu.VMEM((HALF * F, 128), f32),
            pltpu.VMEM((HALF * F, 128), f32),
            pltpu.VMEM((HALF * F, 128), f32),
            pltpu.VMEM((PAIRS * F, 128), f32),
            pltpu.VMEM((2 * HALF, F * CELLS), f32),
            pltpu.VMEM((2 * HALF * F, 128), f32),
            pltpu.VMEM((3, KEEP, F * CELLS), f32),
            pltpu.VMEM((2, KEEP, F * CELLS), f32),
            pltpu.VMEM((SLOTS + 1, F, 128), f32),
            pltpu.VMEM((3, GIVE, F * CELLS), f32),
        ]
    sem = pltpu.SemaphoreType.DMA
    shapes = {
        "small": (5,), "out": (n, 2), "w": (W_PARTS,), "own": (n,), "xs": (n, 2), "xr": (n, 2),
        "hs": (n,), "hr": (n, SECS - 1), "oss": (n, SECS - 1, 2), "orr": (n, 2), "osl": (n, 2),
        "s1s": (n, STEPS), "s1r": (n, STEPS), "ys": (n, STEPS), "yr": (n, STEPS),
        "s2s": (n, STEPS), "s2r": (n, STEPS), "bs": (n, 2, 3), "br": (n, 2, 2),
        "gs": (n, 2, 3, SECS - 1), "gr": (n, 2, 3),
    }
    scratch += [sem(shape) for shape in shapes.values()]
    anywhere = pl.BlockSpec(memory_space=pl.ANY)
    return pl.pallas_call(
        kernel,
        out_shape=jax.ShapeDtypeStruct((1, TILES, WIDE), f32),
        in_specs=[anywhere] * 6,
        out_specs=anywhere,
        scratch_shapes=scratch,
        compiler_params=pltpu.CompilerParams(
            collective_id=0, has_side_effects=True, vmem_limit_bytes=56 * 2**20
        ),
    )(
        surface,
        weights,
        src_tiles.T,
        block_count[None],
        land_sea,
        exchange_coef[None],
    )


def solution(mesh):
    placed = (
        P("sec", "tile", None),
        P("tile", None, None),
        P("tile", None),
        P("tile"),
        P("tile", None),
        P(),
    )
    return jax.shard_map(
        on_device, mesh=mesh, in_specs=placed, out_specs=P("sec", "tile", None), check_vma=False
    )
```

```python
import functools
import jax
import jax.numpy as jnp
from jax import lax
from jax.experimental import pallas as pl
from jax.experimental.pallas import tpu as pltpu
from jax.sharding import PartitionSpec as P

MESH = pl.DeviceIdType.MESH
FIELDS, CELLS, BLOCKS, TILES = 40, 64, 8, 64
WIDE = FIELDS * CELLS
BANDS, SECS = 64, 4
KEEP = 48
GIVE = TILES - KEEP
SLOTS = 3 * KEEP
PAIRS = TILES // 2
HALF = PAIRS // 2
STEPS = 2
STEP = HALF // STEPS
CHUNKS = (16, 24)
W_PARTS = 8
RING = 4
f32, bf16 = jnp.float32, jnp.bfloat16


def split(x):
    hi = x.astype(bf16).astype(f32)
    return hi, x - hi


def kernel(x_ref, w_ref, ids_ref, used_ref, land_ref, coef_ref, out_ref, *scratch):
    n = len(CHUNKS)
    (wraw, wp, mix, hot, cb, fac, rel, res) = scratch[:8]
    (ids, used, land, coef_in, index, idx, wet, coef) = scratch[8:16]
    per = scratch[16 : 16 + 12 * n]
    (small, out_sem, w_sem, own_sem, xs, xr, hs, hr, oss, orr, osl, s1s, s1r, ys, yr, s2s, s2r, bs, br, gs, gr) = (
        scratch[16 + 12 * n :]
    )
    band_in, part, sib, ysum, yrec, flux, oc, ocd, tot, rec, src, given = [
        [per[12 * i + j] for i in range(n)] for j in range(12)
    ]
    s, b = lax.axis_index("sec"), lax.axis_index("tile")
    core = lax.rem(s, 2)
    mate = s + 1 - 2 * core
    opp = lax.rem(s + 2, SECS)
    east, west = lax.rem(b + 1, BANDS), lax.rem(b + BANDS - 1, BANDS)
    taker = s == SECS - 1
    x = lax.rem(b, RING)
    east_sec = jnp.where(x == RING - 1, opp, s)
    west_sec = jnp.where(x == 0, opp, s)
    lane = lax.broadcasted_iota(jnp.int32, (1, 128), 1)
    low = lane < CELLS
    starts = [sum(CHUNKS[:i]) for i in range(n)]

    def remote(a, z, ss, rs, to):
        return pltpu.make_async_remote_copy(
            src_ref=a, dst_ref=z, send_sem=ss, recv_sem=rs, device_id=to, device_id_type=MESH
        )

    def lanes(i):
        return pl.ds(starts[i] * CELLS, CHUNKS[i] * CELLS)

    per_w = TILES // W_PARTS
    w_copy = [
        pltpu.make_async_copy(
            w_ref.at[pl.ds(i * per_w, per_w)], wraw.at[pl.ds(i * per_w, per_w)], w_sem.at[i]
        )
        for i in range(W_PARTS)
    ]
    keep_rows, give_rows = pl.ds(0, KEEP), pl.ds(KEEP, GIVE)
    own_copy = [
        pltpu.make_async_copy(x_ref.at[0, keep_rows, lanes(i)], band_in[i].at[1], own_sem.at[i])
        for i in range(n)
    ]

    def to_neighbours(i, block):
        return (
            remote(block, band_in[i].at[0], xs.at[i, 0], xr.at[i, 0], (east_sec, east)),
            remote(block, band_in[i].at[2], xs.at[i, 1], xr.at[i, 1], (west_sec, west)),
        )

    def hand_over(i, who):
        return remote(
            x_ref.at[0, give_rows, lanes(i)],
            band_in[i].at[1, pl.ds(pl.multiple_of(who * GIVE, GIVE), GIVE)],
            hs.at[i],
            hr.at[i, who],
            (SECS - 1, b),
        )

    def ocean_to(i, who, z):
        return remote(
            x_ref.at[0, pl.ds((who % 2) * HALF + z * PAIRS, HALF), lanes(i)],
            oc[i].at[pl.ds(z * HALF, HALF)],
            oss.at[i, who, z],
            orr.at[i, z],
            (who, b),
        )

    def ocean_own(i, z):
        return pltpu.make_async_copy(
            x_ref.at[0, pl.ds(HALF + z * PAIRS, HALF), lanes(i)],
            oc[i].at[pl.ds(z * HALF, HALF)],
            osl.at[i, z],
        )

    tables = [
        pltpu.make_async_copy(a, z, small.at[j])
        for j, (a, z) in enumerate(
            ((ids_ref, ids), (used_ref, used), (land_ref, land), (coef_ref, coef_in))
        )
    ]

    barrier = pltpu.get_barrier_semaphore()
    for q in (1, 2, 3):
        pl.semaphore_signal(
            barrier, inc=1, device_id=(lax.rem(s + q, SECS), b), device_id_type=MESH
        )
    for z in (east, west):
        for q in range(SECS):
            pl.semaphore_signal(
                barrier, inc=1, device_id=(lax.rem(s + q, SECS), z), device_id_type=MESH
            )
    for c in tables:
        c.start()
    for c in w_copy:
        c.start()

    @pl.when(jnp.logical_not(taker))
    def _():
        for i in range(n):
            own_copy[i].start()

    @pl.when(taker)
    def _():
        for i in range(n):
            for z in range(2):
                ocean_own(i, z).start()

    pl.semaphore_wait(barrier, 3 * SECS - 1)

    @pl.when(jnp.logical_not(taker))
    def _():
        for i in range(n):
            hand_over(i, s).start()
        for i in range(n):
            for c in to_neighbours(i, x_ref.at[0, keep_rows, lanes(i)]):
                c.start()

    def take_over(i):
        @pl.when(taker)
        def _():
            for who in range(SECS - 1):
                hand_over(i, who).wait_recv()
            for c in to_neighbours(i, band_in[i].at[1]):
                c.start()

    def prepare(t, _):
        for k in range(BLOCKS):
            hi, lo = split(wraw[t, pl.ds(k, CELLS // 2, stride=BLOCKS), :])
            left = jnp.where(low, hi, pltpu.roll(lo, CELLS, 1))
            right = jnp.where(low, pltpu.roll(hi, CELLS, 1), lo)
            mix[k, pl.ds(0, CELLS // 2, stride=2), :] = left
            mix[k, pl.ds(1, CELLS // 2, stride=2), :] = right
        for k in range(BLOCKS):
            wp[t, pl.ds(k * CELLS, CELLS), :] = mix[k].astype(bf16)
        return 0

    def prepare_part(i):
        w_copy[i].wait()
        lax.fori_loop(i * per_w, (i + 1) * per_w, prepare, 0, unroll=4)

    @pl.when(taker)
    def _():
        for i in range(n):
            for who in range(SECS - 1):
                for z in range(2):
                    ocean_to(i, who, z).start()

    take_over(0)

    for c in tables:
        c.wait()
    sec_tiles = BANDS * TILES
    source = ids[...] // sec_tiles
    within = ids[...] % sec_tiles
    slot = (within // TILES - b + 1 + BANDS) % BANDS
    row = within % TILES
    kept = row < KEEP
    owner = jnp.where(kept, source, SECS - 1)
    local = jnp.where(kept, row, source * GIVE + row - KEEP)
    holder = jnp.where(slot == 0, west_sec, jnp.where(slot == 2, east_sec, s))
    valid = lax.broadcasted_iota(jnp.int32, (BLOCKS, TILES), 0) < used[...]
    named = jnp.where(valid & (owner == holder), slot * KEEP + local, SLOTS)
    index[...] = jnp.concatenate([named, named], axis=1)
    to_smem = pltpu.make_async_copy(index, idx, small.at[len(tables)])
    to_smem.start()
    rows = lax.broadcasted_iota(jnp.int32, (SLOTS, 128), 0)
    for kpar in range(2):
        for h in range(2):
            k = 4 * h + kpar
            named = jnp.where(low, index[pl.ds(k, 1), :], index[pl.ds(k + 2, 1), :])
            at = pl.ds(128 * (2 * kpar + h), 128)
            hot[:, at] = jnp.where(rows == named, 1.0, 0.0).astype(bf16)
    dry = land[...].astype(f32)
    wet[...] = jnp.concatenate([dry[:PAIRS], dry[PAIRS:]], axis=1)
    square = [lax.broadcasted_iota(jnp.int32, (FIELDS, FIELDS), d) for d in range(2)]
    diagonal = jnp.where(square[0] == square[1], coef_in[...], 0.0)
    coef[...] = jnp.broadcast_to(jnp.sum(diagonal, axis=1, keepdims=True), (FIELDS, 128))

    for i in range(W_PARTS):
        prepare_part(i)
        if i + 1 < n:
            take_over(i + 1)
    to_smem.wait()

    def spread(view, count, F, dst, base):
        for g in range(count // 8):
            for j in range(F // 2):
                v = view[pl.ds(8 * g, 8), pl.ds(128 * j, 128)]
                r = pltpu.roll(v, CELLS, 1)
                at = (base + 8 * g) * F + 2 * j
                dst[pl.ds(at, 8, stride=F), :] = jnp.where(low, v, r)
                dst[pl.ds(at + 1, 8, stride=F), :] = jnp.where(low, r, v)

    def forward(i):
        F = CHUNKS[i]

        @pl.when(jnp.logical_not(taker))
        def _():
            own_copy[i].wait()

        src[i][SLOTS] = jnp.zeros((F, 128), f32)
        flat = src[i].reshape((SLOTS + 1) * F, 128)
        spread(band_in[i].at[1], KEEP, F, flat, KEEP)
        if i + 1 == n:
            for later in range(1, n):
                prepare_ocean(later)
        arrivals = to_neighbours(i, band_in[i].at[1])
        arrivals[0].wait_recv()
        spread(band_in[i].at[0], KEEP, F, flat, 0)
        arrivals[1].wait_recv()
        spread(band_in[i].at[2], KEEP, F, flat, 2 * KEEP)

        def pair(p, _):
            q = []
            for tp in range(2):
                t = p + PAIRS * tp
                cols = []
                for kp in range(BLOCKS // 2):
                    g0 = idx[2 * kp, t]
                    g1 = idx[2 * kp + 1, t]
                    cols.append(
                        jnp.where(
                            low,
                            src[i][g0],
                            src[i][g1],
                        )
                    )
                hi, lo = split(jnp.concatenate(cols, axis=1))
                lhs = jnp.concatenate([hi, lo], axis=0).astype(bf16)
                o = jnp.dot(lhs, wp[t], preferred_element_type=f32)
                q.append(o[:F] + pltpu.roll(o[:F], CELLS, 1) + o[F:])
            part[i][pl.ds(pl.multiple_of(p * F, 8), F), :] = jnp.where(
                low, q[0], pltpu.roll(q[1], CELLS, 1)
            )
            return 0

        def other(q, _):
            lax.fori_loop(
                0, STEP, lambda u, c: pair((1 - core) * HALF + q * STEP + u, c), 0, unroll=STEP
            )
            sib_copy(i, q).start()
            return 0

        def own(q, _):
            lax.fori_loop(
                0, STEP, lambda u, c: pair(core * HALF + q * STEP + u, c), 0, unroll=STEP
            )
            at = step_rows(i, q)
            sib_copy(i, q).wait_recv()
            ysum[i][at, :] = part[i][half_rows(i, core, q), :] + sib[i][at, :]
            y_copy(i, q).start()
            return 0

        lax.fori_loop(0, STEPS, other, 0)
        lax.fori_loop(0, STEPS, own, 0)

    def step_rows(i, q):
        size = STEP * CHUNKS[i]
        return pl.ds(pl.multiple_of(q * size, 8), size)

    def half_rows(i, which, q):
        size = STEP * CHUNKS[i]
        return pl.ds(pl.multiple_of((which * STEPS + q) * size, 8), size)

    def sib_copy(i, q):
        return remote(
            part[i].at[half_rows(i, 1 - core, q)],
            sib[i].at[step_rows(i, q)],
            s1s.at[i, q],
            s1r.at[i, q],
            (mate, b),
        )

    def y_copy(i, q):
        at = step_rows(i, q)
        return remote(ysum[i].at[at], yrec[i].at[at], ys.at[i, q], yr.at[i, q], (opp, b))

    def flux_copy(i, which, q):
        at = flux[i].at[half_rows(i, which, q)]
        return remote(at, at, s2s.at[i, q], s2r.at[i, q], (mate, b))

    def prepare_ocean(i):
        @pl.when(taker)
        def _():
            for z in range(2):
                ocean_own(i, z).wait()

        @pl.when(jnp.logical_not(taker))
        def _():
            for z in range(2):
                ocean_to(i, 0, z).wait_recv()

        spread(oc[i], 2 * HALF, CHUNKS[i], ocd[i], 0)

    def fluxes(i, q):
        F = CHUNKS[i]
        y_copy(i, q).wait_recv()
        for v in range(STEP):
            u = q * STEP + v
            at = pl.ds(pl.multiple_of(u * F, 8), F)
            a = ocd[i][at, :]
            z = ocd[i][pl.ds(pl.multiple_of((HALF + u) * F, 8), F), :]
            rel[at, :] = ysum[i][at, :] + yrec[i][at, :] - jnp.where(low, a, z)
        here = pl.ds(pl.multiple_of(q * STEP, 8), STEP)
        if i == 0:
            r0, r1, r2 = [rel[pl.ds(q * STEP * F + f, STEP, stride=F), :] for f in range(3)]
            speed = jnp.sqrt(r0 * r0 + r1 * r1 + 0.25)
            stab = 1.0 + 0.5 * jnp.tanh(-r2)
            sea = wet[pl.ds(pl.multiple_of(core * HALF + q * STEP, 8), STEP), :]
            fac[here, :] = speed * stab * sea
        exchange = coef[pl.ds(starts[i], F), :]
        for v in range(STEP):
            u = q * STEP + v
            at = pl.ds(pl.multiple_of(u * F, 8), F)
            to = pl.ds(pl.multiple_of((core * HALF + u) * F, 8), F)
            flux[i][to, :] = exchange * fac[pl.ds(u, 1), :] * rel[at, :]
        flux_copy(i, core, q).start()

    def backward(i):
        F = CHUNKS[i]

        def pair(p, _):
            v = flux[i][pl.ds(pl.multiple_of(p * F, 8), F), :]
            r = pltpu.roll(v, CELLS, 1)
            for tp in range(2):
                t = p + PAIRS * tp
                hi, lo = split(jnp.where(low, v, r) if tp == 0 else jnp.where(low, r, v))
                lhs = jnp.concatenate([hi, lo], axis=0).astype(bf16)
                o = lax.dot_general(
                    lhs, wp[t], (((1,), (1,)), ((), ())), preferred_element_type=f32
                )
                o = o[:F] + o[F:]
                for kp in range(BLOCKS // 2):
                    at = pl.multiple_of((kp * TILES + t) * F, 8)
                    cb[pl.ds(at, F), :] = o[:, 128 * kp : 128 * kp + 128]
            return 0

        def own(q, _):
            fluxes(i, q)
            lax.fori_loop(
                0, STEP, lambda u, c: pair(core * HALF + q * STEP + u, c), 0, unroll=STEP
            )
            return 0

        def other(q, _):
            flux_copy(i, 1 - core, q).wait_recv()
            lax.fori_loop(
                0, STEP, lambda u, c: pair((1 - core) * HALF + q * STEP + u, c), 0, unroll=STEP
            )
            return 0

        lax.fori_loop(0, STEPS, own, 0)
        lax.fori_loop(0, STEPS, other, 0)

        def gather(j, _):
            count = TILES * BLOCKS // 2
            x0 = cb[pl.ds(2 * j, count, stride=F), :]
            x1 = cb[pl.ds(2 * j + 1, count, stride=F), :]
            top = jnp.where(low, x0, pltpu.roll(x1, CELLS, 1))
            bottom = jnp.where(low, pltpu.roll(x0, CELLS, 1), x1)
            hi, lo = split(jnp.concatenate([top, bottom], axis=0))
            rhs = jnp.concatenate([hi, lo], axis=1).astype(bf16)
            o = jnp.dot(hot[...], rhs, preferred_element_type=f32)
            o = o[:, :128] + o[:, 128:]
            at = pl.ds(pl.multiple_of(128 * j, 128), 128)
            for z in range(3):
                tot[i][z, :, at] = o[z * KEEP : (z + 1) * KEEP]
            return 0

        for g in range(2):
            lax.fori_loop(g * F // 4, (g + 1) * F // 4, gather, 0, unroll=F // 4)
            for when, c in back_copies(i, g):
                pl.when(when)(c.start)

    def back_copies(i, g):
        size = CHUNKS[i] * CELLS // 2
        at = pl.ds(g * size, size)
        copies = []
        for o, sec, to in ((0, west_sec, west), (2, east_sec, east), (1, s, b)):
            if o != 1:
                z = (2 - o) // 2
                c = remote(
                    tot[i].at[o, :, at],
                    rec[i].at[z, :, at],
                    bs.at[i, g, o],
                    br.at[i, g, z],
                    (sec, to),
                )
                copies.append((sec != SECS - 1, c))
            for who in range(SECS - 1):
                c = remote(
                    tot[i].at[o, pl.ds(GIVE * who, GIVE), at],
                    given[i].at[2 - o, :, at],
                    gs.at[i, g, o, who],
                    gr.at[i, g, 2 - o],
                    (who, to),
                )
                copies.append((sec == SECS - 1, c))
        return copies

    def back_arrivals(i, g):
        size = CHUNKS[i] * CELLS // 2
        at = pl.ds(g * size, size)
        copies = []
        for z in range(2):
            block = rec[i].at[z, :, at]
            copies.append(remote(block, block, bs.at[i, g, 0], br.at[i, g, z], (opp, b)))
        for z in range(3):
            block = given[i].at[z, :, at]
            copies.append(remote(block, block, bs.at[i, g, 0], gr.at[i, g, z], (opp, b)))
        return copies

    def ocean_out(i):
        F = CHUNKS[i]
        for g in range(PAIRS // 8):
            for j in range(F // 2):
                x0 = flux[i][pl.ds(8 * g * F + 2 * j, 8, stride=F), :]
                x1 = flux[i][pl.ds(8 * g * F + 2 * j + 1, 8, stride=F), :]
                at = pl.ds(starts[i] * CELLS + 128 * j, 128)
                res[pl.ds(8 * g, 8), at] = jnp.where(low, x0, pltpu.roll(x1, CELLS, 1))
                res[pl.ds(PAIRS + 8 * g, 8), at] = jnp.where(
                    low, pltpu.roll(x0, CELLS, 1), x1
                )

    def out_copy(i, g):
        size = CHUNKS[i] * CELLS // 2
        at = pl.ds(starts[i] * CELLS + g * size, size)
        return pltpu.make_async_copy(res.at[:, at], out_ref.at[0, :, at], out_sem.at[i, g])

    def finish(i, g):
        size = CHUNKS[i] * CELLS // 2
        at, to = pl.ds(g * size, size), pl.ds(starts[i] * CELLS + g * size, size)
        for c in back_arrivals(i, g):
            c.wait_recv()
        res[keep_rows, to] = tot[i][1, :, at] + rec[i][0, :, at] + rec[i][1, :, at]
        res[give_rows, to] = given[i][0, :, at] + given[i][1, :, at] + given[i][2, :, at]
        out_copy(i, g).start()

    for i in range(n):
        forward(i)
        if i == 0:
            prepare_ocean(i)
    for i in range(n):
        backward(i)

    @pl.when(taker)
    def _():
        for i in range(n):
            ocean_out(i)
            for g in range(2):
                out_copy(i, g).start()

    @pl.when(jnp.logical_not(taker))
    def _():
        for i in range(n):
            for g in range(2):
                finish(i, g)

    for i in range(n):
        for c in to_neighbours(i, band_in[i].at[1]):
            c.wait_send()
        for q in range(STEPS):
            sib_copy(i, q).wait_send()
            y_copy(i, q).wait_send()
            flux_copy(i, core, q).wait_send()
        for g in range(2):
            out_copy(i, g).wait()
            for when, c in back_copies(i, g):
                pl.when(when)(c.wait_send)

    @pl.when(taker)
    def _():
        for i in range(n):
            for who in range(SECS - 1):
                for z in range(2):
                    ocean_to(i, who, z).wait_send()

    @pl.when(jnp.logical_not(taker))
    def _():
        for i in range(n):
            hand_over(i, s).wait_send()


def on_device(surface, remap_weights, src_tiles, block_count, land_sea, exchange_coef):
    n = len(CHUNKS)
    weights = (
        remap_weights.reshape(TILES, BLOCKS, CELLS // 2, 128)
        .transpose(0, 2, 1, 3)
        .reshape(TILES, BLOCKS * CELLS // 2, 128)
    )
    top = max(CHUNKS)
    scratch = [
        pltpu.VMEM((TILES, BLOCKS * CELLS // 2, 128), f32),
        pltpu.VMEM((TILES, BLOCKS * CELLS, 128), bf16),
        pltpu.VMEM((BLOCKS, CELLS, 128), f32),
        pltpu.VMEM((SLOTS, TILES * BLOCKS), bf16),
        pltpu.VMEM((TILES * BLOCKS // 2 * top, 128), f32),
        pltpu.VMEM((HALF, 128), f32),
        pltpu.VMEM((HALF * top, 128), f32),
        pltpu.VMEM((TILES, WIDE), f32),
        pltpu.VMEM((BLOCKS, TILES), jnp.int32),
        pltpu.VMEM((1, TILES), jnp.int32),
        pltpu.VMEM((TILES, CELLS), jnp.int32),
        pltpu.VMEM((1, FIELDS), f32),
        pltpu.VMEM((BLOCKS, 128), jnp.int32),
        pltpu.SMEM((BLOCKS, 128), jnp.int32),
        pltpu.VMEM((PAIRS, 128), f32),
        pltpu.VMEM((FIELDS, 128), f32),
    ]
    for F in CHUNKS:
        scratch += [
            pltpu.VMEM((3, KEEP, F * CELLS), f32),
            pltpu.VMEM((PAIRS * F, 128), f32),
            pltpu.VMEM((HALF * F, 128), f32),
            pltpu.VMEM((HALF * F, 128), f32),
            pltpu.VMEM((HALF * F, 128), f32),
            pltpu.VMEM((PAIRS * F, 128), f32),
            pltpu.VMEM((2 * HALF, F * CELLS), f32),
            pltpu.VMEM((2 * HALF * F, 128), f32),
            pltpu.VMEM((3, KEEP, F * CELLS), f32),
            pltpu.VMEM((2, KEEP, F * CELLS), f32),
            pltpu.VMEM((SLOTS + 1, F, 128), f32),
            pltpu.VMEM((3, GIVE, F * CELLS), f32),
        ]
    sem = pltpu.SemaphoreType.DMA
    shapes = {
        "small": (5,), "out": (n, 2), "w": (W_PARTS,), "own": (n,), "xs": (n, 2), "xr": (n, 2),
        "hs": (n,), "hr": (n, SECS - 1), "oss": (n, SECS - 1, 2), "orr": (n, 2), "osl": (n, 2),
        "s1s": (n, STEPS), "s1r": (n, STEPS), "ys": (n, STEPS), "yr": (n, STEPS),
        "s2s": (n, STEPS), "s2r": (n, STEPS), "bs": (n, 2, 3), "br": (n, 2, 2),
        "gs": (n, 2, 3, SECS - 1), "gr": (n, 2, 3),
    }
    scratch += [sem(shape) for shape in shapes.values()]
    anywhere = pl.BlockSpec(memory_space=pl.ANY)
    return pl.pallas_call(
        kernel,
        out_shape=jax.ShapeDtypeStruct((1, TILES, WIDE), f32),
        in_specs=[anywhere] * 6,
        out_specs=anywhere,
        scratch_shapes=scratch,
        compiler_params=pltpu.CompilerParams(
            collective_id=0, has_side_effects=True, vmem_limit_bytes=56 * 2**20
        ),
    )(
        surface,
        weights,
        src_tiles.T,
        block_count[None],
        land_sea,
        exchange_coef[None],
    )


def solution(mesh):
    placed = (
        P("sec", "tile", None),
        P("tile", None, None),
        P("tile", None),
        P("tile"),
        P("tile", None),
        P(),
    )
    return jax.shard_map(
        on_device, mesh=mesh, in_specs=placed, out_specs=P("sec", "tile", None), check_vma=False
    )
```
